256 devices in a mesh: ta: 4 (over y), gz: 8 (over x, core), xy: 8 (over z).
Axes of the slice: x: 4, y: 4, z: 8, core: 2. Of those that a mesh axis runs over, the one named last changes fastest.
Arguments:
- right_side: float32 [8, 16, 16, 4, 1152], P('ta', 'gz', 'xy'), may hold values from -6 to 6
- link_blocks: bfloat16 [5, 8, 16, 16, 4, 96, 96], P(None, 'ta', 'gz', 'xy'), may hold values from -0.3125 to 0.3125
Outputs:
- solution: float32 [8, 16, 16, 4, 1152], P('ta', 'gz', 'xy')
- residual: float32 [8, 16, 16, 4, 1152], P('ta', 'gz', 'xy')
The draws below stay inside these ranges and needn't reach their ends.
All inputs are finite; a program needn't handle non-finite values.
Results may differ from the reference program's by a relative error of at most 0.0069.
Values may be sent and summed in bfloat16 or wider, within the bound.
No kernel may reach another device: no remote copies, remote signals or barrier semaphores. Data moves between devices by JAX's collectives and lax.ppermute only.
A program may use at most 64 MiB of HBM per device.

```python
import jax
import jax.numpy as jnp
from jax import lax

COMP = 96
RHS = 12
ITERS = 4
NY = 4
NT = 8
NZ = 16
NX = 16


def shard_levels(key, shape, shards, low, top_value):
    factor_of, own = 1.0, jax.random.fold_in(key, 6)
    for dim, shards_of in shards:
        heights = jnp.exp(jax.random.uniform(jax.random.fold_in(own, dim), (shards_of,), jnp.float32, low / len(shards), top_value / len(shards)))
        factor_of = factor_of * jnp.repeat(heights, shape[dim] // shards_of).reshape([-1 if axis == dim else 1 for axis in range(len(shape))])
    return factor_of


def scatter_about(rng, dims, width, most, pieces=(), kind=jnp.bfloat16):
    entries = width * jax.random.normal(rng, dims, jnp.float32)
    if pieces:
        entries = entries * shard_levels(rng, dims, pieces, -0.22, 0.18)
    return jnp.clip(entries, -most, most).astype(kind)


def setup_inputs(seed: int = 0) -> dict:
    keys = jax.random.split(jax.random.key(seed), 3)
    return {
        "right_side": scatter_about(keys[0], (NT, NZ, NX, NY, RHS * COMP), 1.0, 6.0, ((0, 4), (1, 8), (2, 8)), jnp.float32),
        "link_blocks": scatter_about(keys[1], (5, NT, NZ, NX, NY, COMP, COMP), (4 * COMP) ** -0.5, 0.3125, ((1, 4), (2, 8), (3, 8))),
    }


mass_term = 6.0
forward_form = 'zxyab,zxyrb->zxyra'
adjoint_form = 'zxyba,zxyrb->zxyra'

def multiply(blocks, cells, pattern):

    def single(pair):
        return jnp.einsum(pattern, pair[0].astype(jnp.float32), pair[1].astype(jnp.float32))
    return lax.map(single, (blocks, cells))

def operate(vector, link_blocks):
    shaped = (NT, NZ, NX, NY, RHS, COMP)
    cells = vector.astype(jnp.bfloat16).reshape(shaped)
    summed = mass_term * vector.reshape(shaped) + multiply(link_blocks[0], cells, forward_form)
    for direction in range(4):
        ahead = jnp.roll(cells, -1, direction)
        summed = summed - multiply(link_blocks[direction + 1], ahead, forward_form)
        summed = summed - jnp.roll(multiply(link_blocks[direction + 1], cells, adjoint_form), 1, direction)
    return summed.reshape(vector.shape)

def inner_product(left, right):
    return lax.optimization_barrier(jnp.sum((left * right).reshape(-1, RHS, COMP), axis=(0, 2)))

def scaled(vector, factor):
    return (vector.reshape(vector.shape[:-1] + (RHS, COMP)) * factor[:, None]).reshape(vector.shape)

def reference(right_side, link_blocks):
    solution = jnp.zeros_like(right_side)
    residual = right_side
    saved_q = []
    saved_z = []
    for outer in range(ITERS):
        search = residual
        image = operate(search, link_blocks)
        for earlier in range(outer):
            beta = inner_product(saved_q[earlier], image)
            image = image - scaled(saved_q[earlier], beta)
            search = search - scaled(saved_z[earlier], beta)
        square = inner_product(image, image)
        correlation = inner_product(image, residual)
        length = jnp.sqrt(square + 1e-06)
        alpha = correlation / length
        image = scaled(image, 1.0 / length)
        search = scaled(search, 1.0 / length)
        solution = solution + scaled(search, alpha)
        residual = residual - scaled(image, alpha)
        saved_q.append(image)
        saved_z.append(search)
    return (solution, residual)
```

```python
import functools

import jax
import jax.numpy as jnp
from jax import lax
from jax.experimental import pallas as pl
from jax.experimental.pallas import tpu as pltpu
from jax.sharding import PartitionSpec as P

COMP = 96
RHS = 12
ROWS = 16
ITERS = 4
BASIS = ITERS + 1
mass_term = 6.0
SHIFT = 1.6
EXTENT = (2, 2, 2, 4)
SITES = 32
FACE = 16
ENTRIES = [(i, j) for j in range(BASIS) for i in range(j + 1)]
LANES = len(ENTRIES) * ROWS
DEVICES = 256
AXES = ("ta", "gz", "xy")
KEEP_SQUARE = 1e-4
KEEP_VECTOR = 0.1

NT = (((1,), (1,)), ((), ()))
NN = (((1,), (0,)), ((), ()))
TN = (((0,), (0,)), ((), ()))

CELLS = [(t, z, x, y) for t in range(2) for z in range(2) for x in range(2) for y in range(4)]


def place(cell):
    t, z, x, y = cell
    return ((t * 2 + z) * 2 + x) * 4 + y


def moved(cell, direction, by):
    cell = list(cell)
    cell[direction] = (cell[direction] + by) % EXTENT[direction]
    return tuple(cell)


def on_face(cell, direction):
    rest = [c for d, c in enumerate(cell) if d != direction]
    return (rest[0] * 2 + rest[1]) * 4 + rest[2]


def dot(left, right, dims):
    return lax.dot_general(left, right, dims, preferred_element_type=jnp.float32)


def send_faces(narrow_ref, links_ref, firsts, products):
    for direction in range(3):
        for cell in CELLS:
            site, spot = place(cell), on_face(cell, direction)
            if cell[direction] == 0:
                firsts[direction][spot] = narrow_ref[site]
            else:
                firsts_product = dot(narrow_ref[site], links_ref[(direction + 1) * SITES + site], NN)
                products[direction][spot] = firsts_product.astype(jnp.bfloat16)


def begin_kernel(right_ref, links_ref, wide_ref, narrow_ref, *faces):
    for site in range(SITES):
        wide_ref[site] = jnp.zeros((ROWS, COMP), jnp.float32)
        wide_ref[site, 0:RHS] = right_ref[site]
    for site in range(SITES):
        narrow_ref[site] = wide_ref[site].astype(jnp.bfloat16)
    send_faces(narrow_ref, links_ref, faces[0:3], faces[3:6])


def gram_rows(wides, last):
    return [sum(wides[i][site] * wides[last][site] for site in range(SITES)) for i in range(last + 1)]


def inner_kernel(step, narrow_ref, links_ref, *refs):
    wides, (part_ref, gram_ref) = refs[: step + 1], refs[step + 1 :]
    for cell in CELLS:
        site = place(cell)
        total = dot(narrow_ref[site], links_ref[site], NT)
        for direction in range(4):
            block = (direction + 1) * SITES
            if direction == 3 or cell[direction] == 0:
                total -= dot(narrow_ref[place(moved(cell, direction, 1))], links_ref[block + site], NT)
            if direction == 3 or cell[direction] == 1:
                behind = place(moved(cell, direction, -1))
                total -= dot(narrow_ref[behind], links_ref[block + behind], NN)
        if step:
            total -= SHIFT * wides[step - 1][site]
        part_ref[site] = total
    for i, row in enumerate(gram_rows(wides, step)):
        gram_ref[i] = row


def joined(cell, part_ref, links_ref, ahead, behind):
    site = place(cell)
    total = part_ref[site]
    for direction in range(3):
        spot = on_face(cell, direction)
        if cell[direction] == 1:
            total -= dot(ahead[direction][spot], links_ref[(direction + 1) * SITES + site], NT)
        else:
            total -= behind[direction][spot].astype(jnp.float32)
    return total


def outer_kernel(part_ref, links_ref, *refs):
    ahead, behind, (wide_ref, narrow_ref), faces = refs[0:3], refs[3:6], refs[6:8], refs[8:14]
    for cell in CELLS:
        total = joined(cell, part_ref, links_ref, ahead, behind)
        wide_ref[place(cell)] = total
        narrow_ref[place(cell)] = total.astype(jnp.bfloat16)
    send_faces(narrow_ref, links_ref, faces[0:3], faces[3:6])


def last_kernel(part_ref, links_ref, *refs):
    ahead, behind, wides, grams = refs[0:3], refs[3:6], refs[6:10], refs[10:14]
    wide_ref, sums_ref = refs[14:16]
    for cell in CELLS:
        wide_ref[place(cell)] = joined(cell, part_ref, links_ref, ahead, behind)
    rows = [gram[i] for gram in grams for i in range(gram.shape[0])]
    rows += gram_rows(tuple(wides) + (wide_ref,), ITERS)
    stacked = jnp.concatenate(rows, 0)
    sums_ref[...] = lax.dot_general(
        jnp.ones((DEVICES, COMP), jnp.float32), stacked, NT,
        precision=lax.Precision.HIGHEST, preferred_element_type=jnp.float32,
    )


def apply_coefficients(z):
    q = [mass_term * v for v in z] + [jnp.zeros_like(z[0])]
    for k, v in enumerate(z):
        q[k + 1] = q[k + 1] + v
        if k:
            q[k - 1] = q[k - 1] + SHIFT * v
    return q


def combine(left, right):
    terms = [a * b for a, b in zip(left, right)]
    return sum(terms[1:], terms[0])


def finish_kernel(gathered_ref, w0, w1, w2, w3, w4, solution_ref, residual_ref, sound_ref):
    wides = (w0, w1, w2, w3, w4)
    summed = lax.dot_general(
        gathered_ref[...], jnp.ones((DEVICES, 128), jnp.float32), TN,
        precision=lax.Precision.HIGHEST, preferred_element_type=jnp.float32,
    )
    gram = {}
    for at, (i, j) in enumerate(ENTRIES):
        gram[i, j] = gram[j, i] = summed[at * ROWS : (at + 1) * ROWS]
    size = {key: jnp.abs(value) for key, value in gram.items()}

    def times_gram(v):
        return [combine(v, [gram[i, j] for j in range(len(v))]) for i in range(BASIS)]

    def worst(v, table):
        v = [jnp.abs(a) for a in v]
        return combine(v, [combine(v, [table[i, j] for j in range(len(v))]) for i in range(len(v))])

    zero = jnp.zeros((ROWS, 128), jnp.float32)
    rho = [zero + 1.0] + [zero] * ITERS
    out = [zero] * ITERS
    saved = []
    margin = zero + 1.0
    for step in range(ITERS):
        z = rho[: step + 1]
        q = apply_coefficients(z)
        h = times_gram(q)
        for q_j, h_j, z_j in saved:
            beta = combine(q_j, h)
            q = [a - beta * b for a, b in zip(q, list(q_j) + [zero] * len(q))]
            h = [a - beta * b for a, b in zip(h, h_j)]
            z = [a - beta * b for a, b in zip(z, list(z_j) + [zero] * len(z))]
        square = combine(q, h)
        margin = jnp.minimum(margin, square - KEEP_SQUARE * worst(q, size))
        scale = lax.rsqrt(jnp.maximum(square, 0.0) + 1e-06)
        alpha = combine(rho, h) * scale
        q = [a * scale for a in q]
        h = [a * scale for a in h]
        z = [a * scale for a in z]
        saved.append((q, h, z))
        out = [a + alpha * b for a, b in zip(out, list(z) + [zero] * ITERS)]
        rho = [a - alpha * b for a, b in zip(rho, list(q) + [zero] * BASIS)]
    for v in (rho, out):
        length = combine(v, times_gram(v))
        margin = jnp.minimum(margin, length - KEEP_VECTOR * combine([a * a for a in v], [gram[i, i] for i in range(len(v))]))
    sound_ref[...] = jnp.where(margin >= 0.0, 1.0, 0.0)

    out = [a[:, 0:COMP] for a in out]
    rho = [a[:, 0:COMP] for a in rho]
    for site in range(SITES):
        held = [w[site] for w in wides]
        solution_ref[site] = combine(out, held)[0:RHS]
        residual_ref[site] = combine(rho, held)[0:RHS]


def shape(dims, dtype=jnp.float32):
    return jax.ShapeDtypeStruct(dims, dtype)


FACES = [shape((FACE, ROWS, COMP), jnp.bfloat16)] * 6
WIDE = shape((SITES, ROWS, COMP))
NARROW = shape((SITES, ROWS, COMP), jnp.bfloat16)


def call(kernel, name, out_shape, operands):
    whole = pl.BlockSpec(memory_space=pltpu.VMEM)
    return pl.pallas_call(
        kernel,
        name=name,
        out_shape=out_shape,
        in_specs=[whole] * len(operands),
        out_specs=[whole] * len(out_shape),
        compiler_params=pltpu.CompilerParams(vmem_limit_bytes=24 * 2**20),
    )(*operands)


def shifted(shard, axis, by):
    length = lax.axis_size(axis)
    return lax.ppermute(shard, axis, [(i, (i + by) % length) for i in range(length)])


def stepwise(right_side, link_blocks):
    shaped = (2, 2, 2, 4, RHS, COMP)
    forward_form, adjoint_form = "tzxyab,tzxyrb->tzxyra", "tzxyba,tzxyrb->tzxyra"

    def multiply(blocks, cells, pattern):
        return jnp.einsum(pattern, blocks, cells, preferred_element_type=jnp.float32)

    def inner_product(left, right):
        return lax.psum(jnp.sum(left * right, axis=(0, 1, 2, 3, 5)), AXES)[:, None]

    out, residual = jnp.zeros(shaped, jnp.float32), right_side.reshape(shaped)
    saved = []
    for step in range(ITERS):
        search = residual
        narrow = search.astype(jnp.bfloat16)
        image = mass_term * search + multiply(link_blocks[0], narrow, forward_form)
        for direction in range(4):
            blocks = link_blocks[direction + 1]
            product = multiply(blocks, narrow, adjoint_form)
            if direction == 3:
                ahead, behind = jnp.roll(narrow, -1, 3), jnp.roll(product, 1, 3)
            else:
                axis = AXES[direction]
                first = lax.slice_in_dim(narrow, 0, 1, axis=direction)
                last = lax.slice_in_dim(product, 1, 2, axis=direction)
                rest = lax.slice_in_dim(narrow, 1, 2, axis=direction)
                front = lax.slice_in_dim(product, 0, 1, axis=direction)
                ahead = jnp.concatenate([rest, shifted(first, axis, -1)], direction)
                behind = jnp.concatenate([shifted(last, axis, 1), front], direction)
            image = image - multiply(blocks, ahead, forward_form) - behind
        for q_j, z_j in saved:
            beta = inner_product(q_j, image)
            image = image - q_j * beta
            search = search - z_j * beta
        length = jnp.sqrt(inner_product(image, image) + 1e-06)
        alpha = inner_product(image, residual) / length
        image, search = image / length, search / length
        out = out + search * alpha
        residual = residual - image * alpha
        saved.append((image, search))
    return out.reshape(right_side.shape), residual.reshape(right_side.shape)


def local(right_side, link_blocks):
    links = link_blocks.reshape(5 * SITES, COMP, COMP)
    first = right_side.reshape(SITES, RHS, COMP)
    wide, narrow, *faces = call(begin_kernel, "begin", [WIDE, NARROW] + FACES, (first, links))
    wides, grams = [wide], []
    for step in range(ITERS):
        ahead = [shifted(faces[d], AXES[d], -1) for d in range(3)]
        behind = [shifted(faces[3 + d], AXES[d], 1) for d in range(3)]
        part, gram = call(
            functools.partial(inner_kernel, step), f"inner{step}",
            [WIDE, shape((step + 1, ROWS, COMP))], (narrow, links, *wides),
        )
        grams.append(gram)
        if step < ITERS - 1:
            wide, narrow, *faces = call(
                outer_kernel, f"outer{step}", [WIDE, NARROW] + FACES, (part, links, *ahead, *behind)
            )
        else:
            wide, sums = call(
                last_kernel, "last", [WIDE, shape((DEVICES, LANES))],
                (part, links, *ahead, *behind, *wides, *grams),
            )
        wides.append(wide)
    gathered = lax.all_to_all(sums.reshape(DEVICES, 1, LANES), AXES, 0, 0).reshape(DEVICES, LANES)
    out, residual, sound = call(
        finish_kernel, "finish", [shape((SITES, RHS, COMP))] * 2 + [shape((ROWS, 128))], (gathered, *wides)
    )
    return lax.cond(
        jnp.min(sound) > 0.5,
        lambda: (out.reshape(right_side.shape), residual.reshape(right_side.shape)),
        lambda: stepwise(right_side, link_blocks),
    )


def solution(mesh):
    return jax.shard_map(
        local,
        mesh=mesh,
        in_specs=(P("ta", "gz", "xy", None, None), P(None, "ta", "gz", "xy", None, None, None)),
        out_specs=(P("ta", "gz", "xy", None, None), P("ta", "gz", "xy", None, None)),
        check_vma=False,
    )
```

```python
import functools

import jax
import jax.numpy as jnp
from jax import lax
from jax.experimental import pallas as pl
from jax.experimental.pallas import tpu as pltpu
from jax.sharding import PartitionSpec as P

COMP = 96
RHS = 12
ROWS = 16
ITERS = 4
BASIS = ITERS + 1
mass_term = 6.0
SHIFT = 1.6
EXTENT = (2, 2, 2, 4)
SITES = 32
FACE = 16
GROUPS = 8
ENTRIES = [(i, j) for j in range(BASIS) for i in range(j + 1)]
LANES = len(ENTRIES) * ROWS
FIRST_GROUP = 8
SECOND_GROUP = 32
AXES = ("ta", "gz", "xy")
KEEP_SQUARE = 1e-4
KEEP_VECTOR = 0.1

NT = (((1,), (1,)), ((), ()))
NN = (((1,), (0,)), ((), ()))
TN = (((0,), (0,)), ((), ()))

CELLS = [(t, z, x, y) for t in range(2) for z in range(2) for x in range(2) for y in range(4)]


def place(cell):
    t, z, x, y = cell
    return ((t * 2 + z) * 2 + x) * 4 + y


def moved(cell, direction, by):
    cell = list(cell)
    cell[direction] = (cell[direction] + by) % EXTENT[direction]
    return tuple(cell)


def on_face(cell, direction):
    rest = [c for d, c in enumerate(cell) if d != direction]
    return (rest[0] * 2 + rest[1]) * 4 + rest[2]


def dot(left, right, dims):
    return lax.dot_general(left, right, dims, preferred_element_type=jnp.float32)


def begin_kernel(right_ref, wide_ref, narrow_ref, *firsts):
    wide_ref[...] = jnp.zeros(wide_ref.shape, jnp.float32)
    for group in range(GROUPS):
        row = right_ref[group]
        for source in range(RHS):
            piece = row[:, source * COMP : (source + 1) * COMP]
            for y in range(4):
                wide_ref[group * 4 + y, source : source + 1] = piece[y : y + 1]
    for site in range(SITES):
        narrow_ref[site] = wide_ref[site].astype(jnp.bfloat16)
    send_firsts(narrow_ref, firsts)


def send_firsts(narrow_ref, firsts):
    for direction in range(3):
        for cell in CELLS:
            if cell[direction] == 0:
                firsts[direction][on_face(cell, direction)] = narrow_ref[place(cell)]


def send_products(narrow_ref, links_ref, *products):
    for direction in range(3):
        for cell in CELLS:
            if cell[direction] == 1:
                site = place(cell)
                product = dot(narrow_ref[site], links_ref[(direction + 1) * SITES + site], NN)
                products[direction][on_face(cell, direction)] = product.astype(jnp.bfloat16)


def gram_rows(wides, last):
    return [sum(wides[i][site] * wides[last][site] for site in range(SITES)) for i in range(last + 1)]


def as_rows(wide_ref, row_ref):
    for group in range(GROUPS):
        sites = [wide_ref[group * 4 + y] for y in range(4)]
        pieces = [
            jnp.concatenate([site[source : source + 1] for site in sites], 0) for source in range(RHS)
        ]
        row_ref[group] = jnp.concatenate(pieces, 1)


def inner_kernel(step, narrow_ref, links_ref, *refs):
    wides, (part_ref, gram_ref), row_refs = refs[: step + 1], refs[step + 1 : step + 3], refs[step + 3 :]
    for cell in CELLS:
        site = place(cell)
        total = dot(narrow_ref[site], links_ref[site], NT)
        for direction in range(4):
            block = (direction + 1) * SITES
            if direction == 3 or cell[direction] == 0:
                total -= dot(narrow_ref[place(moved(cell, direction, 1))], links_ref[block + site], NT)
            if direction == 3 or cell[direction] == 1:
                behind = place(moved(cell, direction, -1))
                total -= dot(narrow_ref[behind], links_ref[block + behind], NN)
        if step:
            total -= SHIFT * wides[step - 1][site]
        part_ref[site] = total
    for i, row in enumerate(gram_rows(wides, step)):
        gram_ref[i] = row
    for row_ref in row_refs:
        as_rows(wides[step], row_ref)


def joined(cell, part_ref, links_ref, ahead, behind):
    site = place(cell)
    total = part_ref[site]
    for direction in range(3):
        spot = on_face(cell, direction)
        if cell[direction] == 1:
            total -= dot(ahead[direction][spot], links_ref[(direction + 1) * SITES + site], NT)
        else:
            total -= behind[direction][spot].astype(jnp.float32)
    return total


def outer_kernel(part_ref, links_ref, *refs):
    ahead, behind, (wide_ref, narrow_ref), faces = refs[0:3], refs[3:6], refs[6:8], refs[8:14]
    for cell in CELLS:
        total = joined(cell, part_ref, links_ref, ahead, behind)
        wide_ref[place(cell)] = total
        narrow_ref[place(cell)] = total.astype(jnp.bfloat16)
    send_firsts(narrow_ref, faces[0:3])
    send_products(narrow_ref, links_ref, *faces[3:6])


def last_kernel(part_ref, links_ref, *refs):
    ahead, behind, wides, grams = refs[0:3], refs[3:6], refs[6:10], refs[10:14]
    row_ref, sums_ref, wide_ref = refs[14:17]
    for cell in CELLS:
        wide_ref[place(cell)] = joined(cell, part_ref, links_ref, ahead, behind)
    rows = [gram[i] for gram in grams for i in range(gram.shape[0])]
    rows += gram_rows(tuple(wides) + (wide_ref,), ITERS)
    stacked = jnp.concatenate(rows, 0)
    sums_ref[...] = lax.dot_general(
        jnp.ones((FIRST_GROUP, COMP), jnp.float32), stacked, NT,
        precision=lax.Precision.HIGHEST, preferred_element_type=jnp.float32,
    )
    as_rows(wide_ref, row_ref)


def apply_coefficients(z):
    q = [mass_term * v for v in z] + [jnp.zeros_like(z[0])]
    for k, v in enumerate(z):
        q[k + 1] = q[k + 1] + v
        if k:
            q[k - 1] = q[k - 1] + SHIFT * v
    return q


def combine(left, right):
    terms = [a * b for a, b in zip(left, right)]
    return sum(terms[1:], terms[0])


def finish_kernel(gathered_ref, w0, w1, w2, w3, w4, solution_ref, residual_ref, sound_ref):
    wides = (w0, w1, w2, w3, w4)
    summed = lax.dot_general(
        gathered_ref[...], jnp.ones((SECOND_GROUP, 128), jnp.float32), TN,
        precision=lax.Precision.HIGHEST, preferred_element_type=jnp.float32,
    )
    gram = {}
    for at, (i, j) in enumerate(ENTRIES):
        gram[i, j] = gram[j, i] = summed[at * ROWS : (at + 1) * ROWS]
    size = {key: jnp.abs(value) for key, value in gram.items()}

    def times_gram(v):
        return [combine(v, [gram[i, j] for j in range(len(v))]) for i in range(BASIS)]

    def worst(v, table):
        v = [jnp.abs(a) for a in v]
        return combine(v, [combine(v, [table[i, j] for j in range(len(v))]) for i in range(len(v))])

    zero = jnp.zeros((ROWS, 128), jnp.float32)
    rho = [zero + 1.0] + [zero] * ITERS
    out = [zero] * ITERS
    saved = []
    margin = zero + 1.0
    for step in range(ITERS):
        z = rho[: step + 1]
        q = apply_coefficients(z)
        h = times_gram(q)
        for q_j, h_j, z_j in saved:
            beta = combine(q_j, h)
            q = [a - beta * b for a, b in zip(q, list(q_j) + [zero] * len(q))]
            h = [a - beta * b for a, b in zip(h, h_j)]
            z = [a - beta * b for a, b in zip(z, list(z_j) + [zero] * len(z))]
        square = combine(q, h)
        margin = jnp.minimum(margin, square - KEEP_SQUARE * worst(q, size))
        scale = lax.rsqrt(jnp.maximum(square, 0.0) + 1e-06)
        alpha = combine(rho, h) * scale
        q = [a * scale for a in q]
        h = [a * scale for a in h]
        z = [a * scale for a in z]
        saved.append((q, h, z))
        out = [a + alpha * b for a, b in zip(out, list(z) + [zero] * ITERS)]
        rho = [a - alpha * b for a, b in zip(rho, list(q) + [zero] * BASIS)]
    for v in (rho, out):
        length = combine(v, times_gram(v))
        margin = jnp.minimum(margin, length - KEEP_VECTOR * combine([a * a for a in v], [gram[i, i] for i in range(len(v))]))
    sound_ref[0, 0] = jnp.where(jnp.min(margin) >= 0.0, 1, 0)

    lane = lax.broadcasted_iota(jnp.int32, (ROWS, 128), 1)
    packed = zero
    for at, v in enumerate(out + rho):
        packed = jnp.where(lane == at, v, packed)
    owner = lax.broadcasted_iota(jnp.int32, (ROWS, RHS * COMP), 1)
    low = lax.broadcasted_iota(jnp.int32, (ROWS, RHS * COMP), 0) * COMP
    spread = jnp.where((owner >= low) & (owner < low + COMP), 1.0, 0.0)
    factors = lax.dot_general(
        packed[:, 0:ROWS], spread, TN, precision=lax.Precision.HIGHEST, preferred_element_type=jnp.float32
    )
    for group in range(GROUPS):
        held = [w[group] for w in wides]
        solution_ref[group] = combine([factors[i : i + 1] for i in range(ITERS)], held)
        residual_ref[group] = combine([factors[ITERS + i : ITERS + i + 1] for i in range(BASIS)], held)


def shape(dims, dtype=jnp.float32):
    return jax.ShapeDtypeStruct(dims, dtype)


FACES = [shape((FACE, ROWS, COMP), jnp.bfloat16)] * 3
ROW = shape((GROUPS, 4, RHS * COMP))
WIDE = shape((SITES, ROWS, COMP))
NARROW = shape((SITES, ROWS, COMP), jnp.bfloat16)


def call(kernel, name, out_shape, operands, scratch=()):
    whole = pl.BlockSpec(memory_space=pltpu.VMEM)
    scalar = pl.BlockSpec(memory_space=pltpu.SMEM)
    return pl.pallas_call(
        kernel,
        name=name,
        out_shape=out_shape,
        in_specs=[whole] * len(operands),
        out_specs=[scalar if o.shape == (1, 1) else whole for o in out_shape],
        scratch_shapes=scratch,
        compiler_params=pltpu.CompilerParams(vmem_limit_bytes=24 * 2**20),
    )(*operands)


def shifted(shard, axis, by):
    length = lax.axis_size(axis)
    return lax.ppermute(shard, axis, [(i, (i + by) % length) for i in range(length)])


def stepwise(right_side, link_blocks):
    shaped = (2, 2, 2, 4, RHS, COMP)
    forward_form, adjoint_form = "tzxyab,tzxyrb->tzxyra", "tzxyba,tzxyrb->tzxyra"

    def multiply(blocks, cells, pattern):
        return jnp.einsum(pattern, blocks, cells, preferred_element_type=jnp.float32)

    def inner_product(left, right):
        return lax.psum(jnp.sum(left * right, axis=(0, 1, 2, 3, 5)), AXES)[:, None]

    out, residual = jnp.zeros(shaped, jnp.float32), right_side.reshape(shaped)
    saved = []
    for step in range(ITERS):
        search = residual
        narrow = search.astype(jnp.bfloat16)
        image = mass_term * search + multiply(link_blocks[0], narrow, forward_form)
        for direction in range(4):
            blocks = link_blocks[direction + 1]
            product = multiply(blocks, narrow, adjoint_form)
            if direction == 3:
                ahead, behind = jnp.roll(narrow, -1, 3), jnp.roll(product, 1, 3)
            else:
                axis = AXES[direction]
                first = lax.slice_in_dim(narrow, 0, 1, axis=direction)
                last = lax.slice_in_dim(product, 1, 2, axis=direction)
                rest = lax.slice_in_dim(narrow, 1, 2, axis=direction)
                front = lax.slice_in_dim(product, 0, 1, axis=direction)
                ahead = jnp.concatenate([rest, shifted(first, axis, -1)], direction)
                behind = jnp.concatenate([shifted(last, axis, 1), front], direction)
            image = image - multiply(blocks, ahead, forward_form) - behind
        for q_j, z_j in saved:
            beta = inner_product(q_j, image)
            image = image - q_j * beta
            search = search - z_j * beta
        length = jnp.sqrt(inner_product(image, image) + 1e-06)
        alpha = inner_product(image, residual) / length
        image, search = image / length, search / length
        out = out + search * alpha
        residual = residual - image * alpha
        saved.append((image, search))
    return out.reshape(right_side.shape), residual.reshape(right_side.shape)


def local(right_side, link_blocks):
    links = link_blocks.reshape(5 * SITES, COMP, COMP)
    row = right_side.reshape(GROUPS, 4, RHS * COMP)
    wide, narrow, *firsts = call(begin_kernel, "begin", [WIDE, NARROW] + FACES, (row,))
    products = call(send_products, "products", FACES, (narrow, links))
    wides, grams, rows = [wide], [], [row]
    for step in range(ITERS):
        ahead = [shifted(firsts[d], AXES[d], -1) for d in range(3)]
        behind = [shifted(products[d], AXES[d], 1) for d in range(3)]
        part, gram, *made = call(
            functools.partial(inner_kernel, step), f"inner{step}",
            [WIDE, shape((step + 1, ROWS, COMP))] + [ROW] * (step > 0), (narrow, links, *wides),
        )
        grams.append(gram)
        rows += made
        if step < ITERS - 1:
            wide, narrow, *faces = call(
                outer_kernel, f"outer{step}", [WIDE, NARROW] + FACES * 2, (part, links, *ahead, *behind)
            )
            firsts, products = faces[0:3], faces[3:6]
            wides.append(wide)
        else:
            made, sums = call(
                last_kernel, "last", [ROW, shape((FIRST_GROUP, LANES))],
                (part, links, *ahead, *behind, *wides, *grams),
                [pltpu.VMEM((SITES, ROWS, COMP), jnp.float32)],
            )
            rows.append(made)
    sums = jnp.sum(lax.all_to_all(sums, "gz", 0, 0), 0)
    sums = lax.all_to_all(jnp.broadcast_to(sums, (SECOND_GROUP, LANES)), ("ta", "xy"), 0, 0)
    out, residual, sound = call(
        finish_kernel, "finish", [ROW, ROW, shape((1, 1), jnp.int32)], (sums, *rows)
    )
    return lax.cond(
        sound[0, 0] > 0,
        lambda: (out.reshape(right_side.shape), residual.reshape(right_side.shape)),
        lambda: stepwise(right_side, link_blocks),
    )


def solution(mesh):
    return jax.shard_map(
        local,
        mesh=mesh,
        in_specs=(P("ta", "gz", "xy", None, None), P(None, "ta", "gz", "xy", None, None, None)),
        out_specs=(P("ta", "gz", "xy", None, None), P("ta", "gz", "xy", None, None)),
        check_vma=False,
    )
```

```python
import functools

import jax
import jax.numpy as jnp
from jax import lax
from jax.experimental import pallas as pl
from jax.experimental.pallas import tpu as pltpu
from jax.sharding import PartitionSpec as P

COMP = 96
RHS = 12
ROWS = 16
ITERS = 4
BASIS = ITERS + 1
mass_term = 6.0
SHIFT = 1.6
EXTENT = (2, 2, 2, 4)
SITES = 32
FACE = 16
GROUPS = 8
ENTRIES = [(i, j) for j in range(BASIS) for i in range(j + 1)]
LANES = len(ENTRIES) * ROWS
FIRST_GROUP = 8
SECOND_GROUP = 32
AXES = ("ta", "gz", "xy")
ORDER = (0, 2, 1)
KEEP_SQUARE = 1e-4
KEEP_VECTOR = 0.1

LAST_SLICES = [(SITES + 16, 16)]
LAST_SLICES += [(2 * SITES + t * 16 + 8, 8) for t in range(2)]
LAST_SLICES += [(3 * SITES + t * 16 + z * 8 + 4, 4) for t in range(2) for z in range(2)]
OTHER_SLICES = [(0, SITES + 16)]
OTHER_SLICES += [(2 * SITES + t * 16, 8) for t in range(2)]
OTHER_SLICES += [(3 * SITES + t * 16 + z * 8, 4) for t in range(2) for z in range(2)] + [(4 * SITES, SITES)]

NT = (((1,), (1,)), ((), ()))
NN = (((1,), (0,)), ((), ()))
TN = (((0,), (0,)), ((), ()))

CELLS = [(t, z, x, y) for t in range(2) for z in range(2) for x in range(2) for y in range(4)]


def place(cell):
    t, z, x, y = cell
    return ((t * 2 + z) * 2 + x) * 4 + y


def moved(cell, direction, by):
    cell = list(cell)
    cell[direction] = (cell[direction] + by) % EXTENT[direction]
    return tuple(cell)


def on_face(cell, direction):
    rest = [c for d, c in enumerate(cell) if d != direction]
    return (rest[0] * 2 + rest[1]) * 4 + rest[2]


def dot(left, right, dims):
    return lax.dot_general(left, right, dims, preferred_element_type=jnp.float32)


def begin_kernel(right_ref, links_ref, wide_ref, narrow_ref, *refs):
    firsts, products, held_ref, row_ref, sems = refs[0:3], refs[3:6], refs[6], refs[7], refs[8]
    copies = [pltpu.make_async_copy(right_ref, row_ref, sems.at[0])]
    for start, count in LAST_SLICES + OTHER_SLICES:
        here = pl.ds(start, count)
        copies.append(pltpu.make_async_copy(links_ref.at[here], held_ref.at[here], sems.at[len(copies)]))
    for copy in copies:
        copy.start()
    for site in range(SITES):
        wide_ref[site] = jnp.zeros((ROWS, COMP), jnp.float32)
    copies[0].wait()
    for group in range(GROUPS):
        row = row_ref[group]
        for source in range(RHS):
            piece = row[:, source * COMP : (source + 1) * COMP]
            for y in range(4):
                wide_ref[group * 4 + y, source : source + 1] = piece[y : y + 1]
    for site in range(SITES):
        narrow_ref[site] = wide_ref[site].astype(jnp.bfloat16)
    send_firsts(narrow_ref, firsts)
    for copy in copies[1 : len(LAST_SLICES) + 1]:
        copy.wait()
    send_products(narrow_ref, held_ref, products)
    for copy in copies[len(LAST_SLICES) + 1 :]:
        copy.wait()


def send_firsts(narrow_ref, firsts):
    for direction in range(3):
        for cell in CELLS:
            if cell[direction] == 0:
                firsts[direction][on_face(cell, direction)] = narrow_ref[place(cell)]


def send_products(narrow_ref, links_ref, products):
    for direction in range(3):
        for cell in CELLS:
            if cell[direction] == 1:
                site = place(cell)
                spot = on_face(cell, direction)
                product = dot(narrow_ref[site], links_ref[(direction + 1) * SITES + site], NN)
                products[direction][spot] = product.astype(jnp.bfloat16)


def gram_rows(wides, last):
    return [sum(wides[i][site] * wides[last][site] for site in range(SITES)) for i in range(last + 1)]


def as_rows(wide_ref, row_ref, at=0):
    for group in range(GROUPS):
        sites = [wide_ref[group * 4 + y] for y in range(4)]
        pieces = [
            jnp.concatenate([site[source : source + 1] for site in sites], 0) for source in range(RHS)
        ]
        row_ref[at + group] = jnp.concatenate(pieces, 1)


def inner_kernel(step, narrow_ref, links_ref, *refs):
    wides, (part_ref, gram_ref), row_refs = refs[: step + 1], refs[step + 1 : step + 3], refs[step + 3 :]
    for cell in CELLS:
        site = place(cell)
        total = dot(narrow_ref[site], links_ref[site], NT)
        for direction in range(4):
            block = (direction + 1) * SITES
            if direction == 3 or cell[direction] == 0:
                total -= dot(narrow_ref[place(moved(cell, direction, 1))], links_ref[block + site], NT)
            if direction == 3 or cell[direction] == 1:
                behind = place(moved(cell, direction, -1))
                total -= dot(narrow_ref[behind], links_ref[block + behind], NN)
        if step:
            total -= SHIFT * wides[step - 1][site]
        part_ref[site] = total
    for i, row in enumerate(gram_rows(wides, step)):
        gram_ref[i] = row
    for row_ref in row_refs:
        as_rows(wides[step], row_ref)


def middle_kernel(part_ref, links_ref, behind_ref, *refs):
    ahead, next_ref = refs[0:3], refs[3]
    for cell in CELLS:
        site = place(cell)
        total = part_ref[site]
        for direction in range(3):
            if cell[direction] == 1:
                link = links_ref[(direction + 1) * SITES + site]
                total -= dot(ahead[direction][on_face(cell, direction)], link, NT)
        if cell[0] == 0:
            total -= behind_ref[on_face(cell, 0)].astype(jnp.float32)
        next_ref[site] = total


def joined(cell, part_ref, behind):
    total = part_ref[place(cell)]
    for direction in (1, 2):
        if cell[direction] == 0:
            total -= behind[direction - 1][on_face(cell, direction)].astype(jnp.float32)
    return total


def outer_kernel(part_ref, links_ref, *refs):
    behind, (wide_ref, narrow_ref), faces = refs[0:2], refs[2:4], refs[4:10]
    for cell in CELLS:
        total = joined(cell, part_ref, behind)
        wide_ref[place(cell)] = total
        narrow_ref[place(cell)] = total.astype(jnp.bfloat16)
    send_firsts(narrow_ref, faces[0:3])
    send_products(narrow_ref, links_ref, faces[3:6])


def last_kernel(part_ref, *refs):
    behind, wides, grams = refs[0:2], refs[2:6], refs[6:10]
    rows_in, out_ref, wide_ref = refs[10:14], refs[14], refs[15]
    for cell in CELLS:
        wide_ref[place(cell)] = joined(cell, part_ref, behind)
    rows = [gram[i] for gram in grams for i in range(gram.shape[0])]
    rows += gram_rows(tuple(wides) + (wide_ref,), ITERS)
    stacked = jnp.concatenate(rows, 0)
    out_ref[BASIS * GROUPS, 0:1, 0:LANES] = lax.dot_general(
        jnp.ones((8, COMP), jnp.float32), stacked, NT,
        precision=lax.Precision.HIGHEST, preferred_element_type=jnp.float32,
    )[0:1]
    for j, row_ref in enumerate(rows_in):
        out_ref[j * GROUPS : (j + 1) * GROUPS] = row_ref[...]
    as_rows(wide_ref, out_ref, ITERS * GROUPS)


def apply_coefficients(z):
    q = [mass_term * v for v in z] + [jnp.zeros_like(z[0])]
    for k, v in enumerate(z):
        q[k + 1] = q[k + 1] + v
        if k:
            q[k - 1] = q[k - 1] + SHIFT * v
    return q


def combine(left, right):
    terms = [a * b for a, b in zip(left, right)]
    return sum(terms[1:], terms[0])


def finish_kernel(gathered_ref, held_ref, solution_ref, residual_ref, sound_ref):
    summed = lax.dot_general(
        gathered_ref[...], jnp.ones((SECOND_GROUP, 128), jnp.float32), TN,
        precision=lax.Precision.HIGHEST, preferred_element_type=jnp.float32,
    )
    gram = {}
    for at, (i, j) in enumerate(ENTRIES):
        gram[i, j] = gram[j, i] = summed[at * ROWS : (at + 1) * ROWS]
    size = {key: jnp.abs(value) for key, value in gram.items()}

    def times_gram(v):
        return [combine(v, [gram[i, j] for j in range(len(v))]) for i in range(BASIS)]

    def worst(v, table):
        v = [jnp.abs(a) for a in v]
        return combine(v, [combine(v, [table[i, j] for j in range(len(v))]) for i in range(len(v))])

    zero = jnp.zeros((ROWS, 128), jnp.float32)
    rho = [zero + 1.0] + [zero] * ITERS
    out = [zero] * ITERS
    saved = []
    margin = zero + 1.0
    for step in range(ITERS):
        z = rho[: step + 1]
        q = apply_coefficients(z)
        h = times_gram(q)
        for q_j, h_j, z_j in saved:
            beta = combine(q_j, h)
            q = [a - beta * b for a, b in zip(q, list(q_j) + [zero] * len(q))]
            h = [a - beta * b for a, b in zip(h, h_j)]
            z = [a - beta * b for a, b in zip(z, list(z_j) + [zero] * len(z))]
        square = combine(q, h)
        margin = jnp.minimum(margin, square - KEEP_SQUARE * worst(q, size))
        scale = lax.rsqrt(jnp.maximum(square, 0.0) + 1e-06)
        alpha = combine(rho, h) * scale
        q = [a * scale for a in q]
        h = [a * scale for a in h]
        z = [a * scale for a in z]
        saved.append((q, h, z))
        out = [a + alpha * b for a, b in zip(out, list(z) + [zero] * ITERS)]
        rho = [a - alpha * b for a, b in zip(rho, list(q) + [zero] * BASIS)]
    for v in (rho, out):
        length = combine(v, times_gram(v))
        margin = jnp.minimum(margin, length - KEEP_VECTOR * combine([a * a for a in v], [gram[i, i] for i in range(len(v))]))
    sound_ref[0, 0] = jnp.where(jnp.min(margin) >= 0.0, 1, 0)

    lane = lax.broadcasted_iota(jnp.int32, (ROWS, 128), 1)
    packed = zero
    for at, v in enumerate(out + rho):
        packed = jnp.where(lane == at, v, packed)
    owner = lax.broadcasted_iota(jnp.int32, (ROWS, RHS * COMP), 1)
    low = lax.broadcasted_iota(jnp.int32, (ROWS, RHS * COMP), 0) * COMP
    spread = jnp.where((owner >= low) & (owner < low + COMP), 1.0, 0.0)
    factors = lax.dot_general(
        packed[:, 0:ROWS], spread, TN, precision=lax.Precision.HIGHEST, preferred_element_type=jnp.float32
    )
    for group in range(GROUPS):
        held = [held_ref[j * GROUPS + group] for j in range(BASIS)]
        solution_ref[group] = combine([factors[i : i + 1] for i in range(ITERS)], held)
        residual_ref[group] = combine([factors[ITERS + i : ITERS + i + 1] for i in range(BASIS)], held)


def shape(dims, dtype=jnp.float32):
    return jax.ShapeDtypeStruct(dims, dtype)


FACES = [shape((FACE, ROWS, COMP), jnp.bfloat16)] * 3
LINKS = shape((5 * SITES, COMP, COMP), jnp.bfloat16)
ROW = shape((GROUPS, 4, RHS * COMP))
WIDE = shape((SITES, ROWS, COMP))
NARROW = shape((SITES, ROWS, COMP), jnp.bfloat16)


def call(kernel, name, out_shape, operands, scratch=(), apart=()):
    whole = pl.BlockSpec(memory_space=pltpu.VMEM)
    scalar = pl.BlockSpec(memory_space=pltpu.SMEM)
    return pl.pallas_call(
        kernel,
        name=name,
        out_shape=out_shape,
        in_specs=[pl.BlockSpec(memory_space=pl.ANY) if i in apart else whole for i in range(len(operands))],
        out_specs=[scalar if o.shape == (1, 1) else whole for o in out_shape],
        scratch_shapes=scratch,
        compiler_params=pltpu.CompilerParams(vmem_limit_bytes=24 * 2**20),
    )(*operands)


def shifted(shard, axis, by):
    length = lax.axis_size(axis)
    return lax.ppermute(shard, axis, [(i, (i + by) % length) for i in range(length)])


def stepwise(right_side, link_blocks):
    shaped = (2, 2, 2, 4, RHS, COMP)
    forward_form, adjoint_form = "tzxyab,tzxyrb->tzxyra", "tzxyba,tzxyrb->tzxyra"

    def multiply(blocks, cells, pattern):
        return jnp.einsum(pattern, blocks, cells, preferred_element_type=jnp.float32)

    def inner_product(left, right):
        return lax.psum(jnp.sum(left * right, axis=(0, 1, 2, 3, 5)), AXES)[:, None]

    out, residual = jnp.zeros(shaped, jnp.float32), right_side.reshape(shaped)
    saved = []
    for step in range(ITERS):
        search = residual
        narrow = search.astype(jnp.bfloat16)
        image = mass_term * search + multiply(link_blocks[0], narrow, forward_form)
        for direction in range(4):
            blocks = link_blocks[direction + 1]
            product = multiply(blocks, narrow, adjoint_form)
            if direction == 3:
                ahead, behind = jnp.roll(narrow, -1, 3), jnp.roll(product, 1, 3)
            else:
                axis = AXES[direction]
                first = lax.slice_in_dim(narrow, 0, 1, axis=direction)
                last = lax.slice_in_dim(product, 1, 2, axis=direction)
                rest = lax.slice_in_dim(narrow, 1, 2, axis=direction)
                front = lax.slice_in_dim(product, 0, 1, axis=direction)
                ahead = jnp.concatenate([rest, shifted(first, axis, -1)], direction)
                behind = jnp.concatenate([shifted(last, axis, 1), front], direction)
            image = image - multiply(blocks, ahead, forward_form) - behind
        for q_j, z_j in saved:
            beta = inner_product(q_j, image)
            image = image - q_j * beta
            search = search - z_j * beta
        length = jnp.sqrt(inner_product(image, image) + 1e-06)
        alpha = inner_product(image, residual) / length
        image, search = image / length, search / length
        out = out + search * alpha
        residual = residual - image * alpha
        saved.append((image, search))
    return out.reshape(right_side.shape), residual.reshape(right_side.shape)


def local(right_side, link_blocks):
    links = link_blocks.reshape(5 * SITES, COMP, COMP)
    row = right_side.reshape(GROUPS, 4, RHS * COMP)
    wide, narrow, *faces, links = call(
        begin_kernel, "begin", [WIDE, NARROW] + FACES * 2 + [LINKS], (row, links),
        [pltpu.VMEM((GROUPS, 4, RHS * COMP), jnp.float32),
         pltpu.SemaphoreType.DMA((len(LAST_SLICES + OTHER_SLICES) + 1,))],
        apart=(0, 1),
    )
    firsts, products = faces[0:3], faces[3:6]
    wides, grams, rows = [wide], [], [row]
    for step in range(ITERS):
        ahead, behind = [None] * 3, [None] * 3
        for d in ORDER:
            ahead[d] = shifted(firsts[d], AXES[d], -1)
            behind[d] = shifted(products[d], AXES[d], 1)
        part, gram, *made = call(
            functools.partial(inner_kernel, step), f"inner{step}",
            [WIDE, shape((step + 1, ROWS, COMP))] + [ROW] * (step > 0), (narrow, links, *wides),
        )
        grams.append(gram)
        rows += made
        (part,) = call(middle_kernel, f"middle{step}", [WIDE], (part, links, behind[0], *ahead))
        if step < ITERS - 1:
            wide, narrow, *faces = call(
                outer_kernel, f"outer{step}", [WIDE, NARROW] + FACES * 2, (part, links, *behind[1:])
            )
            firsts, products = faces[0:3], faces[3:6]
            wides.append(wide)
        else:
            (held,) = call(
                last_kernel, "last", [shape((BASIS * GROUPS + 1, 4, RHS * COMP))],
                (part, *behind[1:], *wides, *grams, *rows),
                [pltpu.VMEM((SITES, ROWS, COMP), jnp.float32)],
            )
    sums = held[BASIS * GROUPS, 0, 0:LANES]
    for axes, members in (("gz", 8), (("ta", "xy"), 32)):
        sums = lax.all_to_all(jnp.broadcast_to(sums, (members, LANES)), axes, 0, 0)
        if members == 8:
            sums = jnp.sum(sums, 0)
    out, residual, sound = call(
        finish_kernel, "finish", [ROW, ROW, shape((1, 1), jnp.int32)], (sums, held)
    )
    return lax.cond(
        sound[0, 0] > 0,
        lambda: (out.reshape(right_side.shape), residual.reshape(right_side.shape)),
        lambda: stepwise(right_side, link_blocks),
    )


def solution(mesh):
    return jax.shard_map(
        local,
        mesh=mesh,
        in_specs=(P("ta", "gz", "xy", None, None), P(None, "ta", "gz", "xy", None, None, None)),
        out_specs=(P("ta", "gz", "xy", None, None), P("ta", "gz", "xy", None, None)),
        check_vma=False,
    )
```

```python
import functools

import jax
import jax.numpy as jnp
from jax import lax
from jax.experimental import pallas as pl
from jax.experimental.pallas import tpu as pltpu
from jax.sharding import PartitionSpec as P

COMP = 96
RHS = 12
ROWS = 16
ITERS = 4
BASIS = ITERS + 1
mass_term = 6.0
SHIFT = 1.6
EXTENT = (2, 2, 2, 4)
SITES = 32
FACE = 16
BLOCKS = 12
GROUPS = 8
ENTRIES = [(i, j) for j in range(BASIS) for i in range(j + 1)]
LANES = len(ENTRIES) * ROWS
FIRST_GROUP = 8
SECOND_GROUP = 32
AXES = ("ta", "gz", "xy")
ORDER = (0, 2, 1)
KEEP_SQUARE = 1e-4
KEEP_VECTOR = 0.1

LAST_SLICES = [(SITES + 16, 16)]
LAST_SLICES += [(2 * SITES + t * 16 + 8, 8) for t in range(2)]
LAST_SLICES += [(3 * SITES + t * 16 + z * 8 + 4, 4) for t in range(2) for z in range(2)]
OTHER_SLICES = [(0, SITES + 16)]
OTHER_SLICES += [(2 * SITES + t * 16, 8) for t in range(2)]
OTHER_SLICES += [(3 * SITES + t * 16 + z * 8, 4) for t in range(2) for z in range(2)] + [(4 * SITES, SITES)]

NT = (((1,), (1,)), ((), ()))
NN = (((1,), (0,)), ((), ()))
TN = (((0,), (0,)), ((), ()))

CELLS = [(t, z, x, y) for t in range(2) for z in range(2) for x in range(2) for y in range(4)]


def place(cell):
    t, z, x, y = cell
    return ((t * 2 + z) * 2 + x) * 4 + y


def moved(cell, direction, by):
    cell = list(cell)
    cell[direction] = (cell[direction] + by) % EXTENT[direction]
    return tuple(cell)


def on_face(cell, direction):
    rest = [c for d, c in enumerate(cell) if d != direction]
    return (rest[0] * 2 + rest[1]) * 4 + rest[2]


def dot(left, right, dims):
    return lax.dot_general(left, right, dims, preferred_element_type=jnp.float32)


def begin_kernel(right_ref, links_ref, wide_ref, narrow_ref, *refs):
    firsts, products, held_ref, row_ref, sems = refs[0:3], refs[3:6], refs[6], refs[7], refs[8]
    copies = [pltpu.make_async_copy(right_ref, row_ref, sems.at[0])]
    for start, count in LAST_SLICES + OTHER_SLICES:
        here = pl.ds(start, count)
        copies.append(pltpu.make_async_copy(links_ref.at[here], held_ref.at[here], sems.at[len(copies)]))
    for copy in copies:
        copy.start()
    for site in range(SITES):
        wide_ref[site] = jnp.zeros((ROWS, COMP), jnp.float32)
    copies[0].wait()
    for group in range(GROUPS):
        row = row_ref[group]
        for source in range(RHS):
            piece = row[:, source * COMP : (source + 1) * COMP]
            for y in range(4):
                wide_ref[group * 4 + y, source : source + 1] = piece[y : y + 1]
    for site in range(SITES):
        narrow_ref[site] = wide_ref[site].astype(jnp.bfloat16)
    send_firsts(wide_ref, firsts)
    for copy in copies[1 : len(LAST_SLICES) + 1]:
        copy.wait()
    send_products(narrow_ref, held_ref, products)
    for copy in copies[len(LAST_SLICES) + 1 :]:
        copy.wait()


def in_face_order(direction, side):
    return [c for c in CELLS if c[direction] == side]


def send_firsts(wide_ref, firsts):
    for direction in range(3):
        packed(firsts[direction], [wide_ref[place(c)] for c in in_face_order(direction, 0)])


def send_products(narrow_ref, links_ref, products):
    for direction in range(3):
        sites = [place(c) for c in in_face_order(direction, 1)]
        block = (direction + 1) * SITES
        packed(products[direction], [dot(narrow_ref[s], links_ref[block + s], NN) for s in sites])


def gram_rows(wides, last):
    return [sum(wides[i][site] * wides[last][site] for site in range(SITES)) for i in range(last + 1)]


def as_rows(wide_ref, row_ref, at=0):
    for group in range(GROUPS):
        sites = [wide_ref[group * 4 + y] for y in range(4)]
        pieces = [
            jnp.concatenate([site[source : source + 1] for site in sites], 0) for source in range(RHS)
        ]
        row_ref[at + group] = jnp.concatenate(pieces, 1)


def inner_kernel(step, narrow_ref, links_ref, *refs):
    wides, (part_ref, gram_ref), row_refs = refs[: step + 1], refs[step + 1 : step + 3], refs[step + 3 :]
    for cell in CELLS:
        site = place(cell)
        turned = dot(links_ref[site], narrow_ref[site], NT)
        for direction in range(4):
            if direction == 3 or cell[direction] == 0:
                ahead = narrow_ref[place(moved(cell, direction, 1))]
                turned -= dot(links_ref[(direction + 1) * SITES + site], ahead, NT)
        total = turned.T
        for direction in range(4):
            if direction == 3 or cell[direction] == 1:
                behind = place(moved(cell, direction, -1))
                total -= dot(narrow_ref[behind], links_ref[(direction + 1) * SITES + behind], NN)
        if step:
            total -= SHIFT * wides[step - 1][site]
        part_ref[site] = total
    for i, row in enumerate(gram_rows(wides, step)):
        gram_ref[i] = row
    for row_ref in row_refs:
        as_rows(wides[step], row_ref)


def middle_kernel(part_ref, links_ref, behind_ref, *refs):
    ahead = [[v.astype(jnp.bfloat16) for v in unpacked(ref)] for ref in refs[0:3]]
    behind, next_ref = unpacked(behind_ref), refs[3]
    for cell in CELLS:
        site = place(cell)
        total, turned = part_ref[site], None
        for direction in range(3):
            if cell[direction] == 1:
                link = links_ref[(direction + 1) * SITES + site]
                term = dot(link, ahead[direction][on_face(cell, direction)], NT)
                turned = term if turned is None else turned + term
        if turned is not None:
            total -= turned.T
        if cell[0] == 0:
            total -= behind[on_face(cell, 0)]
        next_ref[site] = total


def joined(cell, part_ref, behind):
    total = part_ref[place(cell)]
    for direction, faces in zip((1, 2), behind):
        if cell[direction] == 0:
            total -= faces[on_face(cell, direction)]
    return total


def packed(ref, values):
    for at in range(0, FACE, 4):
        rest = values[at + 3]
        for j in range(3):
            block = jnp.concatenate([values[at + j][0:RHS], rest[4 * j : 4 * j + 4]], 0)
            ref[at // 4 * 3 + j] = block.astype(jnp.bfloat16)


def unpacked(ref):
    values = []
    for at in range(0, BLOCKS, 3):
        blocks = [ref[at + j].astype(jnp.float32) for j in range(3)]
        rest = jnp.concatenate([block[RHS:ROWS] for block in blocks] + [jnp.zeros((4, COMP), jnp.float32)], 0)
        clear = jnp.zeros((ROWS - RHS, COMP), jnp.float32)
        values += [jnp.concatenate([block[0:RHS], clear], 0) for block in blocks] + [rest]
    return values


def outer_kernel(part_ref, links_ref, *refs):
    (wide_ref, narrow_ref), faces = refs[2:4], refs[4:10]
    behind = [unpacked(ref) for ref in refs[0:2]]
    for cell in CELLS:
        total = joined(cell, part_ref, behind)
        wide_ref[place(cell)] = total
        narrow_ref[place(cell)] = total.astype(jnp.bfloat16)
    send_firsts(wide_ref, faces[0:3])
    send_products(narrow_ref, links_ref, faces[3:6])


def last_kernel(part_ref, *refs):
    wides, grams = refs[2:6], refs[6:10]
    behind = [unpacked(ref) for ref in refs[0:2]]
    rows_in, out_ref, wide_ref = refs[10:14], refs[14], refs[15]
    for cell in CELLS:
        wide_ref[place(cell)] = joined(cell, part_ref, behind)
    rows = [gram[i] for gram in grams for i in range(gram.shape[0])]
    rows += gram_rows(tuple(wides) + (wide_ref,), ITERS)
    stacked = jnp.concatenate(rows, 0)
    out_ref[BASIS * GROUPS, 0:1, 0:LANES] = lax.dot_general(
        jnp.ones((8, COMP), jnp.float32), stacked, NT,
        precision=lax.Precision.HIGHEST, preferred_element_type=jnp.float32,
    )[0:1]
    for j, row_ref in enumerate(rows_in):
        out_ref[j * GROUPS : (j + 1) * GROUPS] = row_ref[...]
    as_rows(wide_ref, out_ref, ITERS * GROUPS)


def apply_coefficients(z):
    q = [mass_term * v for v in z] + [jnp.zeros_like(z[0])]
    for k, v in enumerate(z):
        q[k + 1] = q[k + 1] + v
        if k:
            q[k - 1] = q[k - 1] + SHIFT * v
    return q


def combine(left, right):
    terms = [a * b for a, b in zip(left, right)]
    return sum(terms[1:], terms[0])


def finish_kernel(gathered_ref, held_ref, solution_ref, residual_ref, unsound_ref):
    summed = lax.dot_general(
        gathered_ref[...], jnp.ones((SECOND_GROUP, 128), jnp.float32), TN,
        precision=lax.Precision.HIGHEST, preferred_element_type=jnp.float32,
    )
    gram = {}
    for at, (i, j) in enumerate(ENTRIES):
        gram[i, j] = gram[j, i] = summed[at * ROWS : (at + 1) * ROWS]
    size = {key: jnp.abs(value) for key, value in gram.items()}

    def times_gram(v):
        return [combine(v, [gram[i, j] for j in range(len(v))]) for i in range(BASIS)]

    def worst(v, table):
        v = [jnp.abs(a) for a in v]
        return combine(v, [combine(v, [table[i, j] for j in range(len(v))]) for i in range(len(v))])

    zero = jnp.zeros((ROWS, 128), jnp.float32)
    rho = [zero + 1.0] + [zero] * ITERS
    out = [zero] * ITERS
    saved = []
    margin = zero + 1.0
    for step in range(ITERS):
        z = rho[: step + 1]
        q = apply_coefficients(z)
        h = times_gram(q)
        for q_j, h_j, z_j in saved:
            beta = combine(q_j, h)
            q = [a - beta * b for a, b in zip(q, list(q_j) + [zero] * len(q))]
            h = [a - beta * b for a, b in zip(h, h_j)]
            z = [a - beta * b for a, b in zip(z, list(z_j) + [zero] * len(z))]
        square = combine(q, h)
        margin = jnp.minimum(margin, square - KEEP_SQUARE * worst(q, size))
        scale = lax.rsqrt(jnp.maximum(square, 0.0) + 1e-06)
        alpha = combine(rho, h) * scale
        q = [a * scale for a in q]
        h = [a * scale for a in h]
        z = [a * scale for a in z]
        saved.append((q, h, z))
        out = [a + alpha * b for a, b in zip(out, list(z) + [zero] * ITERS)]
        rho = [a - alpha * b for a, b in zip(rho, list(q) + [zero] * BASIS)]
    for v in (rho, out):
        length = combine(v, times_gram(v))
        margin = jnp.minimum(margin, length - KEEP_VECTOR * combine([a * a for a in v], [gram[i, i] for i in range(len(v))]))
    unsound_ref[0, 0] = jnp.where(jnp.min(margin) >= 0.0, 0, 1)

    lane = lax.broadcasted_iota(jnp.int32, (ROWS, 128), 1)
    packed = zero
    for at, v in enumerate(out + rho):
        packed = jnp.where(lane == at, v, packed)
    owner = lax.broadcasted_iota(jnp.int32, (ROWS, RHS * COMP), 1)
    low = lax.broadcasted_iota(jnp.int32, (ROWS, RHS * COMP), 0) * COMP
    spread = jnp.where((owner >= low) & (owner < low + COMP), 1.0, 0.0)
    factors = lax.dot_general(
        packed[:, 0:ROWS], spread, TN, precision=lax.Precision.HIGHEST, preferred_element_type=jnp.float32
    )
    for group in range(GROUPS):
        held = [held_ref[j * GROUPS + group] for j in range(BASIS)]
        solution_ref[group] = combine([factors[i : i + 1] for i in range(ITERS)], held)
        residual_ref[group] = combine([factors[ITERS + i : ITERS + i + 1] for i in range(BASIS)], held)


def shape(dims, dtype=jnp.float32):
    return jax.ShapeDtypeStruct(dims, dtype)


FACES = [shape((BLOCKS, ROWS, COMP), jnp.bfloat16)] * 3
LINKS = shape((5 * SITES, COMP, COMP), jnp.bfloat16)
ROW = shape((GROUPS, 4, RHS * COMP))
WIDE = shape((SITES, ROWS, COMP))
NARROW = shape((SITES, ROWS, COMP), jnp.bfloat16)


def call(kernel, name, out_shape, operands, scratch=(), apart=()):
    whole = pl.BlockSpec(memory_space=pltpu.VMEM)
    scalar = pl.BlockSpec(memory_space=pltpu.SMEM)
    return pl.pallas_call(
        kernel,
        name=name,
        out_shape=out_shape,
        in_specs=[pl.BlockSpec(memory_space=pl.ANY) if i in apart else whole for i in range(len(operands))],
        out_specs=[scalar if o.shape == (1, 1) else whole for o in out_shape],
        scratch_shapes=scratch,
        compiler_params=pltpu.CompilerParams(vmem_limit_bytes=24 * 2**20),
    )(*operands)


def shifted(shard, axis, by):
    length = lax.axis_size(axis)
    return lax.ppermute(shard, axis, [(i, (i + by) % length) for i in range(length)])


def stepwise(right_side, link_blocks):
    shaped = (2, 2, 2, 4, RHS, COMP)
    forward_form, adjoint_form = "tzxyab,tzxyrb->tzxyra", "tzxyba,tzxyrb->tzxyra"

    def multiply(blocks, cells, pattern):
        return jnp.einsum(pattern, blocks, cells, preferred_element_type=jnp.float32)

    def inner_product(left, right):
        return lax.psum(jnp.sum(left * right, axis=(0, 1, 2, 3, 5)), AXES)[:, None]

    out, residual = jnp.zeros(shaped, jnp.float32), right_side.reshape(shaped)
    saved = []
    for step in range(ITERS):
        search = residual
        narrow = search.astype(jnp.bfloat16)
        image = mass_term * search + multiply(link_blocks[0], narrow, forward_form)
        for direction in range(4):
            blocks = link_blocks[direction + 1]
            product = multiply(blocks, narrow, adjoint_form)
            if direction == 3:
                ahead, behind = jnp.roll(narrow, -1, 3), jnp.roll(product, 1, 3)
            else:
                axis = AXES[direction]
                first = lax.slice_in_dim(narrow, 0, 1, axis=direction)
                last = lax.slice_in_dim(product, 1, 2, axis=direction)
                rest = lax.slice_in_dim(narrow, 1, 2, axis=direction)
                front = lax.slice_in_dim(product, 0, 1, axis=direction)
                ahead = jnp.concatenate([rest, shifted(first, axis, -1)], direction)
                behind = jnp.concatenate([shifted(last, axis, 1), front], direction)
            image = image - multiply(blocks, ahead, forward_form) - behind
        for q_j, z_j in saved:
            beta = inner_product(q_j, image)
            image = image - q_j * beta
            search = search - z_j * beta
        length = jnp.sqrt(inner_product(image, image) + 1e-06)
        alpha = inner_product(image, residual) / length
        image, search = image / length, search / length
        out = out + search * alpha
        residual = residual - image * alpha
        saved.append((image, search))
    return out.reshape(right_side.shape), residual.reshape(right_side.shape)


def local(right_side, link_blocks):
    links = link_blocks.reshape(5 * SITES, COMP, COMP)
    row = right_side.reshape(GROUPS, 4, RHS * COMP)
    wide, narrow, *faces, links = call(
        begin_kernel, "begin", [WIDE, NARROW] + FACES * 2 + [LINKS], (row, links),
        [pltpu.VMEM((GROUPS, 4, RHS * COMP), jnp.float32),
         pltpu.SemaphoreType.DMA((len(LAST_SLICES + OTHER_SLICES) + 1,))],
        apart=(0, 1),
    )
    firsts, products = faces[0:3], faces[3:6]
    wides, grams, rows = [wide], [], [row]
    for step in range(ITERS):
        ahead, behind = [None] * 3, [None] * 3
        for d in ORDER:
            ahead[d] = shifted(firsts[d], AXES[d], -1)
            behind[d] = shifted(products[d], AXES[d], 1)
        part, gram, *made = call(
            functools.partial(inner_kernel, step), f"inner{step}",
            [WIDE, shape((step + 1, ROWS, COMP))] + [ROW] * (step > 0), (narrow, links, *wides),
        )
        grams.append(gram)
        rows += made
        (part,) = call(middle_kernel, f"middle{step}", [WIDE], (part, links, behind[0], *ahead))
        if step < ITERS - 1:
            wide, narrow, *faces = call(
                outer_kernel, f"outer{step}", [WIDE, NARROW] + FACES * 2, (part, links, *behind[1:])
            )
            firsts, products = faces[0:3], faces[3:6]
            wides.append(wide)
        else:
            (held,) = call(
                last_kernel, "last", [shape((BASIS * GROUPS + 1, 4, RHS * COMP))],
                (part, *behind[1:], *wides, *grams, *rows),
                [pltpu.VMEM((SITES, ROWS, COMP), jnp.float32)],
            )
    sums = held[BASIS * GROUPS, 0, 0:LANES]
    for axes, members in (("gz", 8), (("ta", "xy"), 32)):
        sums = lax.all_to_all(jnp.broadcast_to(sums, (members, LANES)), axes, 0, 0)
        if members == 8:
            sums = jnp.sum(sums, 0)
    out, residual, unsound = call(
        finish_kernel, "finish", [ROW, ROW, shape((1, 1), jnp.int32)], (sums, held)
    )
    return lax.cond(
        unsound[0, 0] > 0,
        lambda: stepwise(right_side, link_blocks),
        lambda: (out.reshape(right_side.shape), residual.reshape(right_side.shape)),
    )


def solution(mesh):
    return jax.shard_map(
        local,
        mesh=mesh,
        in_specs=(P("ta", "gz", "xy", None, None), P(None, "ta", "gz", "xy", None, None, None)),
        out_specs=(P("ta", "gz", "xy", None, None), P("ta", "gz", "xy", None, None)),
        check_vma=False,
    )
```

```python
import functools

import jax
import jax.numpy as jnp
from jax import lax
from jax.experimental import pallas as pl
from jax.experimental.pallas import tpu as pltpu
from jax.sharding import PartitionSpec as P

COMP = 96
RHS = 12
ROWS = 16
ITERS = 4
BASIS = ITERS + 1
mass_term = 6.0
SHIFT = 1.6
EXTENT = (2, 2, 2, 4)
SITES = 32
FACE = 16
BLOCKS = 12
GROUPS = 8
ENTRIES = [(i, j) for j in range(BASIS) for i in range(j + 1)]
LANES = len(ENTRIES) * ROWS
FIRST_GROUP = 8
SECOND_GROUP = 32
AXES = ("ta", "gz", "xy")
ORDER = (0, 2, 1)
KEEP_SQUARE = 1e-2
KEEP_VECTOR = 0.4

LAST_SLICES = [(SITES + 16, 16)]
LAST_SLICES += [(2 * SITES + t * 16 + 8, 8) for t in range(2)]
LAST_SLICES += [(3 * SITES + t * 16 + z * 8 + 4, 4) for t in range(2) for z in range(2)]
OTHER_SLICES = [(0, SITES + 16)]
OTHER_SLICES += [(2 * SITES + t * 16, 8) for t in range(2)]
OTHER_SLICES += [(3 * SITES + t * 16 + z * 8, 4) for t in range(2) for z in range(2)] + [(4 * SITES, SITES)]

NT = (((1,), (1,)), ((), ()))
NN = (((1,), (0,)), ((), ()))
TN = (((0,), (0,)), ((), ()))

CELLS = [(t, z, x, y) for t in range(2) for z in range(2) for x in range(2) for y in range(4)]


def place(cell):
    t, z, x, y = cell
    return ((t * 2 + z) * 2 + x) * 4 + y


def moved(cell, direction, by):
    cell = list(cell)
    cell[direction] = (cell[direction] + by) % EXTENT[direction]
    return tuple(cell)


def on_face(cell, direction):
    rest = [c for d, c in enumerate(cell) if d != direction]
    return (rest[0] * 2 + rest[1]) * 4 + rest[2]


def dot(left, right, dims):
    return lax.dot_general(left, right, dims, preferred_element_type=jnp.float32)


def begin_kernel(right_ref, links_ref, wide_ref, narrow_ref, *refs):
    firsts, products, held_ref, row_ref, sems = refs[0:3], refs[3:6], refs[6], refs[7], refs[8]
    copies = [pltpu.make_async_copy(right_ref, row_ref, sems.at[0])]
    for start, count in LAST_SLICES + OTHER_SLICES:
        here = pl.ds(start, count)
        copies.append(pltpu.make_async_copy(links_ref.at[here], held_ref.at[here], sems.at[len(copies)]))
    for copy in copies:
        copy.start()
    for site in range(SITES):
        wide_ref[site] = jnp.zeros((ROWS, COMP), jnp.float32)
    copies[0].wait()
    for group in range(GROUPS):
        row = row_ref[group]
        for source in range(RHS):
            piece = row[:, source * COMP : (source + 1) * COMP]
            for y in range(4):
                wide_ref[group * 4 + y, source : source + 1] = piece[y : y + 1]
    for site in range(SITES):
        narrow_ref[site] = wide_ref[site].astype(jnp.bfloat16)
    send_firsts(wide_ref, firsts)
    for copy in copies[1 : len(LAST_SLICES) + 1]:
        copy.wait()
    send_products(narrow_ref, held_ref, products)
    for copy in copies[len(LAST_SLICES) + 1 :]:
        copy.wait()


def in_face_order(direction, side):
    return [c for c in CELLS if c[direction] == side]


def send_firsts(wide_ref, firsts):
    for direction in range(3):
        packed(firsts[direction], [wide_ref[place(c)] for c in in_face_order(direction, 0)])


def send_products(narrow_ref, links_ref, products):
    for direction in range(3):
        sites = [place(c) for c in in_face_order(direction, 1)]
        block = (direction + 1) * SITES
        packed(products[direction], [dot(narrow_ref[s], links_ref[block + s], NN) for s in sites])


def gram_rows(wides, last):
    return [sum(wides[i][site] * wides[last][site] for site in range(SITES)) for i in range(last + 1)]


def as_rows(wide_ref, row_ref, at=0):
    for group in range(GROUPS):
        sites = [wide_ref[group * 4 + y] for y in range(4)]
        pieces = [
            jnp.concatenate([site[source : source + 1] for site in sites], 0) for source in range(RHS)
        ]
        row_ref[at + group] = jnp.concatenate(pieces, 1)


def inner_kernel(step, narrow_ref, links_ref, *refs):
    wides, (part_ref, gram_ref), row_refs = refs[: step + 1], refs[step + 1 : step + 3], refs[step + 3 :]
    for cell in CELLS:
        site = place(cell)
        turned = dot(links_ref[site], narrow_ref[site], NT)
        for direction in range(4):
            if direction == 3 or cell[direction] == 0:
                ahead = narrow_ref[place(moved(cell, direction, 1))]
                turned -= dot(links_ref[(direction + 1) * SITES + site], ahead, NT)
        total = turned.T
        for direction in range(4):
            if direction == 3 or cell[direction] == 1:
                behind = place(moved(cell, direction, -1))
                total -= dot(narrow_ref[behind], links_ref[(direction + 1) * SITES + behind], NN)
        if step:
            total -= SHIFT * wides[step - 1][site]
        part_ref[site] = total
    for i, row in enumerate(gram_rows(wides, step)):
        gram_ref[i] = row
    for row_ref in row_refs:
        as_rows(wides[step], row_ref)


def middle_kernel(part_ref, links_ref, behind_ref, *refs):
    ahead = [[v.astype(jnp.bfloat16) for v in unpacked(ref)] for ref in refs[0:3]]
    behind, next_ref = unpacked(behind_ref), refs[3]
    for cell in CELLS:
        site = place(cell)
        total, turned = part_ref[site], None
        for direction in range(3):
            if cell[direction] == 1:
                link = links_ref[(direction + 1) * SITES + site]
                term = dot(link, ahead[direction][on_face(cell, direction)], NT)
                turned = term if turned is None else turned + term
        if turned is not None:
            total -= turned.T
        if cell[0] == 0:
            total -= behind[on_face(cell, 0)]
        next_ref[site] = total


def joined(cell, part_ref, behind):
    total = part_ref[place(cell)]
    for direction, faces in zip((1, 2), behind):
        if cell[direction] == 0:
            total -= faces[on_face(cell, direction)]
    return total


def packed(ref, values):
    for at in range(0, FACE, 4):
        rest = values[at + 3]
        for j in range(3):
            block = jnp.concatenate([values[at + j][0:RHS], rest[4 * j : 4 * j + 4]], 0)
            ref[at // 4 * 3 + j] = block.astype(jnp.bfloat16)


def unpacked(ref):
    values = []
    for at in range(0, BLOCKS, 3):
        blocks = [ref[at + j].astype(jnp.float32) for j in range(3)]
        rest = jnp.concatenate([block[RHS:ROWS] for block in blocks] + [jnp.zeros((4, COMP), jnp.float32)], 0)
        clear = jnp.zeros((ROWS - RHS, COMP), jnp.float32)
        values += [jnp.concatenate([block[0:RHS], clear], 0) for block in blocks] + [rest]
    return values


def outer_kernel(part_ref, links_ref, *refs):
    (wide_ref, narrow_ref), faces = refs[2:4], refs[4:10]
    behind = [unpacked(ref) for ref in refs[0:2]]
    for cell in CELLS:
        total = joined(cell, part_ref, behind)
        wide_ref[place(cell)] = total
        narrow_ref[place(cell)] = total.astype(jnp.bfloat16)
    send_firsts(wide_ref, faces[0:3])
    send_products(narrow_ref, links_ref, faces[3:6])


def last_kernel(part_ref, *refs):
    wides, grams = refs[2:6], refs[6:10]
    behind = [unpacked(ref) for ref in refs[0:2]]
    rows_in, out_ref, wide_ref = refs[10:14], refs[14], refs[15]
    for cell in CELLS:
        wide_ref[place(cell)] = joined(cell, part_ref, behind)
    rows = [gram[i] for gram in grams for i in range(gram.shape[0])]
    rows += gram_rows(tuple(wides) + (wide_ref,), ITERS)
    stacked = jnp.concatenate(rows, 0)
    out_ref[BASIS * GROUPS, 0:1, 0:LANES] = lax.dot_general(
        jnp.ones((8, COMP), jnp.float32), stacked, NT,
        precision=lax.Precision.HIGHEST, preferred_element_type=jnp.float32,
    )[0:1]
    for j, row_ref in enumerate(rows_in):
        out_ref[j * GROUPS : (j + 1) * GROUPS] = row_ref[...]
    as_rows(wide_ref, out_ref, ITERS * GROUPS)


def apply_coefficients(z):
    q = [mass_term * v for v in z] + [jnp.zeros_like(z[0])]
    for k, v in enumerate(z):
        q[k + 1] = q[k + 1] + v
        if k:
            q[k - 1] = q[k - 1] + SHIFT * v
    return q


def combine(left, right):
    terms = [a * b for a, b in zip(left, right)]
    return sum(terms[1:], terms[0])


def finish_kernel(gathered_ref, held_ref, solution_ref, residual_ref, unsound_ref):
    summed = lax.dot_general(
        gathered_ref[...], jnp.ones((SECOND_GROUP, 128), jnp.float32), TN,
        precision=lax.Precision.HIGHEST, preferred_element_type=jnp.float32,
    )
    gram = {}
    for at, (i, j) in enumerate(ENTRIES):
        gram[i, j] = gram[j, i] = summed[at * ROWS : (at + 1) * ROWS]
    size = {key: jnp.abs(value) for key, value in gram.items()}

    def times_gram(v):
        return [combine(v, [gram[i, j] for j in range(len(v))]) for i in range(BASIS)]

    def worst(v, table):
        v = [jnp.abs(a) for a in v]
        return combine(v, [combine(v, [table[i, j] for j in range(len(v))]) for i in range(len(v))])

    zero = jnp.zeros((ROWS, 128), jnp.float32)
    rho = [zero + 1.0] + [zero] * ITERS
    out = [zero] * ITERS
    saved = []
    margin = zero + 1.0
    for step in range(ITERS):
        z = rho[: step + 1]
        q = apply_coefficients(z)
        h = times_gram(q)
        for q_j, h_j, z_j in saved:
            beta = combine(q_j, h)
            q = [a - beta * b for a, b in zip(q, list(q_j) + [zero] * len(q))]
            h = [a - beta * b for a, b in zip(h, h_j)]
            z = [a - beta * b for a, b in zip(z, list(z_j) + [zero] * len(z))]
        square = combine(q, h)
        margin = jnp.minimum(margin, square - KEEP_SQUARE * worst(q, size))
        scale = lax.rsqrt(jnp.maximum(square, 0.0) + 1e-06)
        alpha = combine(rho, h) * scale
        q = [a * scale for a in q]
        h = [a * scale for a in h]
        z = [a * scale for a in z]
        saved.append((q, h, z))
        out = [a + alpha * b for a, b in zip(out, list(z) + [zero] * ITERS)]
        rho = [a - alpha * b for a, b in zip(rho, list(q) + [zero] * BASIS)]
    for v in (rho, out):
        length = combine(v, times_gram(v))
        margin = jnp.minimum(margin, length - KEEP_VECTOR * combine([a * a for a in v], [gram[i, i] for i in range(len(v))]))
    unsound_ref[0, 0] = jnp.where(jnp.min(margin) >= 0.0, 0, 1)

    lane = lax.broadcasted_iota(jnp.int32, (ROWS, 128), 1)
    packed = zero
    for at, v in enumerate(out + rho):
        packed = jnp.where(lane == at, v, packed)
    owner = lax.broadcasted_iota(jnp.int32, (ROWS, RHS * COMP), 1)
    low = lax.broadcasted_iota(jnp.int32, (ROWS, RHS * COMP), 0) * COMP
    spread = jnp.where((owner >= low) & (owner < low + COMP), 1.0, 0.0)
    factors = lax.dot_general(
        packed[:, 0:ROWS], spread, TN, precision=lax.Precision.HIGHEST, preferred_element_type=jnp.float32
    )
    for group in range(GROUPS):
        held = [held_ref[j * GROUPS + group] for j in range(BASIS)]
        solution_ref[group] = combine([factors[i : i + 1] for i in range(ITERS)], held)
        residual_ref[group] = combine([factors[ITERS + i : ITERS + i + 1] for i in range(BASIS)], held)


def shape(dims, dtype=jnp.float32):
    return jax.ShapeDtypeStruct(dims, dtype)


FACES = [shape((BLOCKS, ROWS, COMP), jnp.bfloat16)] * 3
LINKS = shape((5 * SITES, COMP, COMP), jnp.bfloat16)
ROW = shape((GROUPS, 4, RHS * COMP))
WIDE = shape((SITES, ROWS, COMP))
NARROW = shape((SITES, ROWS, COMP), jnp.bfloat16)


def call(kernel, name, out_shape, operands, scratch=(), apart=()):
    whole = pl.BlockSpec(memory_space=pltpu.VMEM)
    scalar = pl.BlockSpec(memory_space=pltpu.SMEM)
    return pl.pallas_call(
        kernel,
        name=name,
        out_shape=out_shape,
        in_specs=[pl.BlockSpec(memory_space=pl.ANY) if i in apart else whole for i in range(len(operands))],
        out_specs=[scalar if o.shape == (1, 1) else whole for o in out_shape],
        scratch_shapes=scratch,
        compiler_params=pltpu.CompilerParams(vmem_limit_bytes=24 * 2**20),
    )(*operands)


def shifted(shard, axis, by):
    length = lax.axis_size(axis)
    return lax.ppermute(shard, axis, [(i, (i + by) % length) for i in range(length)])


def stepwise(right_side, link_blocks):
    shaped = (2, 2, 2, 4, RHS, COMP)
    forward_form, adjoint_form = "tzxyab,tzxyrb->tzxyra", "tzxyba,tzxyrb->tzxyra"

    def multiply(blocks, cells, pattern):
        return jnp.einsum(pattern, blocks, cells, preferred_element_type=jnp.float32)

    def inner_product(left, right):
        return lax.psum(jnp.sum(left * right, axis=(0, 1, 2, 3, 5)), AXES)[:, None]

    out, residual = jnp.zeros(shaped, jnp.float32), right_side.reshape(shaped)
    saved = []
    for step in range(ITERS):
        search = residual
        narrow = search.astype(jnp.bfloat16)
        image = mass_term * search + multiply(link_blocks[0], narrow, forward_form)
        for direction in range(4):
            blocks = link_blocks[direction + 1]
            product = multiply(blocks, narrow, adjoint_form)
            if direction == 3:
                ahead, behind = jnp.roll(narrow, -1, 3), jnp.roll(product, 1, 3)
            else:
                axis = AXES[direction]
                first = lax.slice_in_dim(narrow, 0, 1, axis=direction)
                last = lax.slice_in_dim(product, 1, 2, axis=direction)
                rest = lax.slice_in_dim(narrow, 1, 2, axis=direction)
                front = lax.slice_in_dim(product, 0, 1, axis=direction)
                ahead = jnp.concatenate([rest, shifted(first, axis, -1)], direction)
                behind = jnp.concatenate([shifted(last, axis, 1), front], direction)
            image = image - multiply(blocks, ahead, forward_form) - behind
        for q_j, z_j in saved:
            beta = inner_product(q_j, image)
            image = image - q_j * beta
            search = search - z_j * beta
        length = jnp.sqrt(inner_product(image, image) + 1e-06)
        alpha = inner_product(image, residual) / length
        image, search = image / length, search / length
        out = out + search * alpha
        residual = residual - image * alpha
        saved.append((image, search))
    return out.reshape(right_side.shape), residual.reshape(right_side.shape)


def local(right_side, link_blocks):
    links = link_blocks.reshape(5 * SITES, COMP, COMP)
    row = right_side.reshape(GROUPS, 4, RHS * COMP)
    wide, narrow, *faces, links = call(
        begin_kernel, "begin", [WIDE, NARROW] + FACES * 2 + [LINKS], (row, links),
        [pltpu.VMEM((GROUPS, 4, RHS * COMP), jnp.float32),
         pltpu.SemaphoreType.DMA((len(LAST_SLICES + OTHER_SLICES) + 1,))],
        apart=(0, 1),
    )
    firsts, products = faces[0:3], faces[3:6]
    wides, grams, rows = [wide], [], [row]
    for step in range(ITERS):
        ahead, behind = [None] * 3, [None] * 3
        for d in ORDER:
            ahead[d] = shifted(firsts[d], AXES[d], -1)
            behind[d] = shifted(products[d], AXES[d], 1)
        part, gram, *made = call(
            functools.partial(inner_kernel, step), f"inner{step}",
            [WIDE, shape((step + 1, ROWS, COMP))] + [ROW] * (step > 0), (narrow, links, *wides),
        )
        grams.append(gram)
        rows += made
        (part,) = call(middle_kernel, f"middle{step}", [WIDE], (part, links, behind[0], *ahead))
        if step < ITERS - 1:
            wide, narrow, *faces = call(
                outer_kernel, f"outer{step}", [WIDE, NARROW] + FACES * 2, (part, links, *behind[1:])
            )
            firsts, products = faces[0:3], faces[3:6]
            wides.append(wide)
        else:
            (held,) = call(
                last_kernel, "last", [shape((BASIS * GROUPS + 1, 4, RHS * COMP))],
                (part, *behind[1:], *wides, *grams, *rows),
                [pltpu.VMEM((SITES, ROWS, COMP), jnp.float32)],
            )
    sums = held[BASIS * GROUPS, 0, 0:LANES]
    for axes, members in (("gz", 8), (("ta", "xy"), 32)):
        sums = lax.all_to_all(jnp.broadcast_to(sums, (members, LANES)), axes, 0, 0)
        if members == 8:
            sums = jnp.sum(sums, 0)
    out, residual, unsound = call(
        finish_kernel, "finish", [ROW, ROW, shape((1, 1), jnp.int32)], (sums, held)
    )
    return lax.cond(
        unsound[0, 0] > 0,
        lambda: stepwise(right_side, link_blocks),
        lambda: (out.reshape(right_side.shape), residual.reshape(right_side.shape)),
    )


def solution(mesh):
    return jax.shard_map(
        local,
        mesh=mesh,
        in_specs=(P("ta", "gz", "xy", None, None), P(None, "ta", "gz", "xy", None, None, None)),
        out_specs=(P("ta", "gz", "xy", None, None), P("ta", "gz", "xy", None, None)),
        check_vma=False,
    )
```

```python
import functools

import jax
import jax.numpy as jnp
from jax import lax
from jax.experimental import pallas as pl
from jax.experimental.pallas import tpu as pltpu
from jax.sharding import PartitionSpec as P

COMP = 96
RHS = 12
ROWS = 16
ITERS = 4
BASIS = ITERS + 1
mass_term = 6.0
SHIFT = 1.6
EXTENT = (2, 2, 2, 4)
SITES = 32
FACE = 16
BLOCKS = 12
GROUPS = 8
ENTRIES = [(i, j) for j in range(BASIS) for i in range(j + 1)]
LANES = len(ENTRIES) * ROWS
FIRST_GROUP = 8
SECOND_GROUP = 32
AXES = ("ta", "gz", "xy")
ORDER = (0, 2, 1)
KEEP_SQUARE = 1e-2
KEEP_VECTOR = 0.4

LAST_SLICES = [(SITES + 16, 16)]
LAST_SLICES += [(2 * SITES + t * 16 + 8, 8) for t in range(2)]
LAST_SLICES += [(3 * SITES + t * 16 + z * 8 + 4, 4) for t in range(2) for z in range(2)]
OTHER_SLICES = [(0, SITES + 16)]
OTHER_SLICES += [(2 * SITES + t * 16, 8) for t in range(2)]
OTHER_SLICES += [(3 * SITES + t * 16 + z * 8, 4) for t in range(2) for z in range(2)] + [(4 * SITES, SITES)]

NT = (((1,), (1,)), ((), ()))
NN = (((1,), (0,)), ((), ()))
TN = (((0,), (0,)), ((), ()))

CELLS = [(t, z, x, y) for t in range(2) for z in range(2) for x in range(2) for y in range(4)]


def place(cell):
    t, z, x, y = cell
    return ((t * 2 + z) * 2 + x) * 4 + y


def moved(cell, direction, by):
    cell = list(cell)
    cell[direction] = (cell[direction] + by) % EXTENT[direction]
    return tuple(cell)


def on_face(cell, direction):
    rest = [c for d, c in enumerate(cell) if d != direction]
    return (rest[0] * 2 + rest[1]) * 4 + rest[2]


def dot(left, right, dims):
    return lax.dot_general(left, right, dims, preferred_element_type=jnp.float32)


def begin_kernel(right_ref, links_ref, wide_ref, narrow_ref, *refs):
    firsts, products, held_ref, row_ref, sems = refs[0:3], refs[3:6], refs[6], refs[7], refs[8]
    copies = [pltpu.make_async_copy(right_ref, row_ref, sems.at[0])]
    for start, count in LAST_SLICES + OTHER_SLICES:
        here = pl.ds(start, count)
        copies.append(pltpu.make_async_copy(links_ref.at[here], held_ref.at[here], sems.at[len(copies)]))
    for copy in copies:
        copy.start()
    for site in range(SITES):
        wide_ref[site] = jnp.zeros((ROWS, COMP), jnp.float32)
    copies[0].wait()
    for group in range(GROUPS):
        row = row_ref[group]
        for source in range(RHS):
            piece = row[:, source * COMP : (source + 1) * COMP]
            for y in range(4):
                wide_ref[group * 4 + y, source : source + 1] = piece[y : y + 1]
    for site in range(SITES):
        narrow_ref[site] = wide_ref[site].astype(jnp.bfloat16)
    send_firsts(wide_ref, firsts)
    for copy in copies[1 : len(LAST_SLICES) + 1]:
        copy.wait()
    send_products(narrow_ref, held_ref, products)
    for copy in copies[len(LAST_SLICES) + 1 :]:
        copy.wait()


def in_face_order(direction, side):
    return [c for c in CELLS if c[direction] == side]


def send_firsts(wide_ref, firsts):
    for direction in range(3):
        packed(firsts[direction], [wide_ref[place(c)] for c in in_face_order(direction, 0)])


def send_products(narrow_ref, links_ref, products):
    for direction in range(3):
        sites = [place(c) for c in in_face_order(direction, 1)]
        block = (direction + 1) * SITES
        packed(products[direction], [dot(narrow_ref[s], links_ref[block + s], NN) for s in sites])


def gram_rows(wides, last):
    return [sum(wides[i][site] * wides[last][site] for site in range(SITES)) for i in range(last + 1)]


def as_rows(wide_ref, row_ref, at=0):
    for group in range(GROUPS):
        sites = [wide_ref[group * 4 + y] for y in range(4)]
        pieces = [
            jnp.concatenate([site[source : source + 1] for site in sites], 0) for source in range(RHS)
        ]
        row_ref[at + group] = jnp.concatenate(pieces, 1)


def inner_kernel(step, narrow_ref, links_ref, *refs):
    wides, (part_ref, gram_ref), row_refs = refs[: step + 1], refs[step + 1 : step + 3], refs[step + 3 :]
    for cell in CELLS:
        site = place(cell)
        turned = dot(links_ref[site], narrow_ref[site], NT)
        for direction in range(4):
            if direction == 3 or cell[direction] == 0:
                ahead = narrow_ref[place(moved(cell, direction, 1))]
                turned -= dot(links_ref[(direction + 1) * SITES + site], ahead, NT)
        total = turned.T
        for direction in range(4):
            if direction == 3 or cell[direction] == 1:
                behind = place(moved(cell, direction, -1))
                total -= dot(narrow_ref[behind], links_ref[(direction + 1) * SITES + behind], NN)
        if step:
            total -= SHIFT * wides[step - 1][site]
        part_ref[site] = total
    for i, row in enumerate(gram_rows(wides, step)):
        gram_ref[i] = row
    for row_ref in row_refs:
        as_rows(wides[step], row_ref)


def middle_kernel(part_ref, links_ref, behind_ref, *refs):
    ahead = [[v.astype(jnp.bfloat16) for v in unpacked(ref)] for ref in refs[0:3]]
    behind, next_ref = unpacked(behind_ref), refs[3]
    for cell in CELLS:
        site = place(cell)
        total, turned = part_ref[site], None
        for direction in range(3):
            if cell[direction] == 1:
                link = links_ref[(direction + 1) * SITES + site]
                term = dot(link, ahead[direction][on_face(cell, direction)], NT)
                turned = term if turned is None else turned + term
        if turned is not None:
            total -= turned.T
        if cell[0] == 0:
            total -= behind[on_face(cell, 0)]
        next_ref[site] = total


def joined(cell, part_ref, behind):
    total = part_ref[place(cell)]
    for direction, faces in zip((1, 2), behind):
        if cell[direction] == 0:
            total -= faces[on_face(cell, direction)]
    return total


def packed(ref, values):
    for at in range(0, FACE, 4):
        rest = values[at + 3]
        for j in range(3):
            block = jnp.concatenate([values[at + j][0:RHS], rest[4 * j : 4 * j + 4]], 0)
            ref[at // 4 * 3 + j] = block.astype(jnp.bfloat16)


def unpacked(ref):
    values = []
    for at in range(0, BLOCKS, 3):
        blocks = [ref[at + j].astype(jnp.float32) for j in range(3)]
        rest = jnp.concatenate([block[RHS:ROWS] for block in blocks] + [jnp.zeros((4, COMP), jnp.float32)], 0)
        clear = jnp.zeros((ROWS - RHS, COMP), jnp.float32)
        values += [jnp.concatenate([block[0:RHS], clear], 0) for block in blocks] + [rest]
    return values


def outer_kernel(part_ref, links_ref, *refs):
    (wide_ref, narrow_ref), faces = refs[2:4], refs[4:10]
    behind = [unpacked(ref) for ref in refs[0:2]]
    for cell in CELLS:
        total = joined(cell, part_ref, behind)
        wide_ref[place(cell)] = total
        narrow_ref[place(cell)] = total.astype(jnp.bfloat16)
    send_firsts(wide_ref, faces[0:3])
    send_products(narrow_ref, links_ref, faces[3:6])


def last_kernel(part_ref, *refs):
    wides, grams = refs[2:6], refs[6:10]
    behind = [unpacked(ref) for ref in refs[0:2]]
    rows_in, out_ref, wide_ref = refs[10:14], refs[14], refs[15]
    for cell in CELLS:
        wide_ref[place(cell)] = joined(cell, part_ref, behind)
    rows = [gram[i] for gram in grams for i in range(gram.shape[0])]
    rows += gram_rows(tuple(wides) + (wide_ref,), ITERS)
    stacked = jnp.concatenate(rows, 0)
    out_ref[BASIS * GROUPS, 0:1, 0:LANES] = lax.dot_general(
        jnp.ones((8, COMP), jnp.float32), stacked, NT,
        precision=lax.Precision.HIGHEST, preferred_element_type=jnp.float32,
    )[0:1]
    for j, row_ref in enumerate(rows_in):
        out_ref[j * GROUPS : (j + 1) * GROUPS] = row_ref[...]
    as_rows(wide_ref, out_ref, ITERS * GROUPS)


def apply_coefficients(z):
    q = [mass_term * v for v in z] + [jnp.zeros_like(z[0])]
    for k, v in enumerate(z):
        q[k + 1] = q[k + 1] + v
        if k:
            q[k - 1] = q[k - 1] + SHIFT * v
    return q


def combine(left, right):
    terms = [a * b for a, b in zip(left, right)]
    while len(terms) > 1:
        terms = [sum(terms[i + 1 : i + 2], terms[i]) for i in range(0, len(terms), 2)]
    return terms[0]


def finish_kernel(gathered_ref, held_ref, solution_ref, residual_ref, unsound_ref, made_ref, sems):
    summed = lax.dot_general(
        gathered_ref[...], jnp.ones((SECOND_GROUP, 128), jnp.float32), TN,
        precision=lax.Precision.HIGHEST, preferred_element_type=jnp.float32,
    )
    gram = {}
    for at, (i, j) in enumerate(ENTRIES):
        gram[i, j] = gram[j, i] = summed[at * ROWS : (at + 1) * ROWS]
    size = {key: jnp.abs(value) for key, value in gram.items()}

    def times_gram(v):
        return [combine(v, [gram[i, j] for j in range(len(v))]) for i in range(BASIS)]

    def worst(v, table):
        v = [jnp.abs(a) for a in v]
        return combine(v, [combine(v, [table[i, j] for j in range(len(v))]) for i in range(len(v))])

    zero = jnp.zeros((ROWS, 128), jnp.float32)
    rho = [zero + 1.0] + [zero] * ITERS
    out = [zero] * ITERS
    saved = []
    margin = zero + 1.0
    for step in range(ITERS):
        z = rho[: step + 1]
        q = apply_coefficients(z)
        h = times_gram(q)
        for q_j, h_j, z_j in saved:
            beta = combine(q_j, h)
            q = [a - beta * b for a, b in zip(q, list(q_j) + [zero] * len(q))]
            h = [a - beta * b for a, b in zip(h, h_j)]
            z = [a - beta * b for a, b in zip(z, list(z_j) + [zero] * len(z))]
        square = combine(q, h)
        margin = jnp.minimum(margin, square - KEEP_SQUARE * worst(q, size))
        scale = lax.rsqrt(jnp.maximum(square, 0.0) + 1e-06)
        alpha = combine(rho, h) * scale
        q = [a * scale for a in q]
        h = [a * scale for a in h]
        z = [a * scale for a in z]
        saved.append((q, h, z))
        out = [a + alpha * b for a, b in zip(out, list(z) + [zero] * ITERS)]
        rho = [a - alpha * b for a, b in zip(rho, list(q) + [zero] * BASIS)]
    for v in (rho, out):
        length = combine(v, times_gram(v))
        margin = jnp.minimum(margin, length - KEEP_VECTOR * combine([a * a for a in v], [gram[i, i] for i in range(len(v))]))
    unsound_ref[0, 0] = jnp.where(jnp.min(margin) >= 0.0, 0, 1)

    lane = lax.broadcasted_iota(jnp.int32, (ROWS, 128), 1)
    packed = zero
    for at, v in enumerate(out + rho):
        packed = jnp.where(lane == at, v, packed)
    owner = lax.broadcasted_iota(jnp.int32, (ROWS, RHS * COMP), 1)
    low = lax.broadcasted_iota(jnp.int32, (ROWS, RHS * COMP), 0) * COMP
    spread = jnp.where((owner >= low) & (owner < low + COMP), 1.0, 0.0)
    factors = lax.dot_general(
        packed[:, 0:ROWS], spread, TN, precision=lax.Precision.HIGHEST, preferred_element_type=jnp.float32
    )
    copies = []
    for half in (0, 4):
        for side, ref in enumerate((solution_ref, residual_ref)):
            count, at = (ITERS, 0) if side == 0 else (BASIS, ITERS)
            weights = [factors[at + i : at + i + 1] for i in range(count)]
            for group in range(half, half + 4):
                made_ref[side, group] = combine(weights, [held_ref[j * GROUPS + group] for j in range(count)])
            here = pl.ds(half, 4)
            copy = pltpu.make_async_copy(made_ref.at[side, here], ref.at[here], sems.at[len(copies)])
            copy.start()
            copies.append(copy)
    for copy in copies:
        copy.wait()


def shape(dims, dtype=jnp.float32):
    return jax.ShapeDtypeStruct(dims, dtype)


FACES = [shape((BLOCKS, ROWS, COMP), jnp.bfloat16)] * 3
LINKS = shape((5 * SITES, COMP, COMP), jnp.bfloat16)
ROW = shape((GROUPS, 4, RHS * COMP))
WIDE = shape((SITES, ROWS, COMP))
NARROW = shape((SITES, ROWS, COMP), jnp.bfloat16)


def call(kernel, name, out_shape, operands, scratch=(), apart=(), out_apart=()):
    whole = pl.BlockSpec(memory_space=pltpu.VMEM)
    scalar = pl.BlockSpec(memory_space=pltpu.SMEM)
    far = pl.BlockSpec(memory_space=pl.ANY)
    return pl.pallas_call(
        kernel,
        name=name,
        out_shape=out_shape,
        in_specs=[pl.BlockSpec(memory_space=pl.ANY) if i in apart else whole for i in range(len(operands))],
        out_specs=[
            far if i in out_apart else scalar if o.shape == (1, 1) else whole for i, o in enumerate(out_shape)
        ],
        scratch_shapes=scratch,
        compiler_params=pltpu.CompilerParams(vmem_limit_bytes=24 * 2**20),
    )(*operands)


def shifted(shard, axis, by):
    length = lax.axis_size(axis)
    return lax.ppermute(shard, axis, [(i, (i + by) % length) for i in range(length)])


def stepwise(right_side, link_blocks):
    shaped = (2, 2, 2, 4, RHS, COMP)
    forward_form, adjoint_form = "tzxyab,tzxyrb->tzxyra", "tzxyba,tzxyrb->tzxyra"

    def multiply(blocks, cells, pattern):
        return jnp.einsum(pattern, blocks, cells, preferred_element_type=jnp.float32)

    def inner_product(left, right):
        return lax.psum(jnp.sum(left * right, axis=(0, 1, 2, 3, 5)), AXES)[:, None]

    out, residual = jnp.zeros(shaped, jnp.float32), right_side.reshape(shaped)
    saved = []
    for step in range(ITERS):
        search = residual
        narrow = search.astype(jnp.bfloat16)
        image = mass_term * search + multiply(link_blocks[0], narrow, forward_form)
        for direction in range(4):
            blocks = link_blocks[direction + 1]
            product = multiply(blocks, narrow, adjoint_form)
            if direction == 3:
                ahead, behind = jnp.roll(narrow, -1, 3), jnp.roll(product, 1, 3)
            else:
                axis = AXES[direction]
                first = lax.slice_in_dim(narrow, 0, 1, axis=direction)
                last = lax.slice_in_dim(product, 1, 2, axis=direction)
                rest = lax.slice_in_dim(narrow, 1, 2, axis=direction)
                front = lax.slice_in_dim(product, 0, 1, axis=direction)
                ahead = jnp.concatenate([rest, shifted(first, axis, -1)], direction)
                behind = jnp.concatenate([shifted(last, axis, 1), front], direction)
            image = image - multiply(blocks, ahead, forward_form) - behind
        for q_j, z_j in saved:
            beta = inner_product(q_j, image)
            image = image - q_j * beta
            search = search - z_j * beta
        length = jnp.sqrt(inner_product(image, image) + 1e-06)
        alpha = inner_product(image, residual) / length
        image, search = image / length, search / length
        out = out + search * alpha
        residual = residual - image * alpha
        saved.append((image, search))
    return out.reshape(right_side.shape), residual.reshape(right_side.shape)


def local(right_side, link_blocks):
    links = link_blocks.reshape(5 * SITES, COMP, COMP)
    row = right_side.reshape(GROUPS, 4, RHS * COMP)
    wide, narrow, *faces, links = call(
        begin_kernel, "begin", [WIDE, NARROW] + FACES * 2 + [LINKS], (row, links),
        [pltpu.VMEM((GROUPS, 4, RHS * COMP), jnp.float32),
         pltpu.SemaphoreType.DMA((len(LAST_SLICES + OTHER_SLICES) + 1,))],
        apart=(0, 1),
    )
    firsts, products = faces[0:3], faces[3:6]
    wides, grams, rows = [wide], [], [row]
    for step in range(ITERS):
        ahead, behind = [None] * 3, [None] * 3
        for d in ORDER:
            ahead[d] = shifted(firsts[d], AXES[d], -1)
            behind[d] = shifted(products[d], AXES[d], 1)
        part, gram, *made = call(
            functools.partial(inner_kernel, step), f"inner{step}",
            [WIDE, shape((step + 1, ROWS, COMP))] + [ROW] * (step > 0), (narrow, links, *wides),
        )
        grams.append(gram)
        rows += made
        (part,) = call(middle_kernel, f"middle{step}", [WIDE], (part, links, behind[0], *ahead))
        if step < ITERS - 1:
            wide, narrow, *faces = call(
                outer_kernel, f"outer{step}", [WIDE, NARROW] + FACES * 2, (part, links, *behind[1:])
            )
            firsts, products = faces[0:3], faces[3:6]
            wides.append(wide)
        else:
            (held,) = call(
                last_kernel, "last", [shape((BASIS * GROUPS + 1, 4, RHS * COMP))],
                (part, *behind[1:], *wides, *grams, *rows),
                [pltpu.VMEM((SITES, ROWS, COMP), jnp.float32)],
            )
    sums = held[BASIS * GROUPS, 0, 0:LANES]
    for axes, members in (("gz", 8), (("ta", "xy"), 32)):
        sums = lax.all_to_all(jnp.broadcast_to(sums, (members, LANES)), axes, 0, 0)
        if members == 8:
            sums = jnp.sum(sums, 0)
    out, residual, unsound = call(
        finish_kernel, "finish", [ROW, ROW, shape((1, 1), jnp.int32)], (sums, held),
        [pltpu.VMEM((2, GROUPS, 4, RHS * COMP), jnp.float32), pltpu.SemaphoreType.DMA((4,))], out_apart=(0, 1),
    )
    return lax.cond(
        unsound[0, 0] > 0,
        lambda: stepwise(right_side, link_blocks),
        lambda: (out.reshape(right_side.shape), residual.reshape(right_side.shape)),
    )


def solution(mesh):
    return jax.shard_map(
        local,
        mesh=mesh,
        in_specs=(P("ta", "gz", "xy", None, None), P(None, "ta", "gz", "xy", None, None, None)),
        out_specs=(P("ta", "gz", "xy", None, None), P("ta", "gz", "xy", None, None)),
        check_vma=False,
    )
```
